32 devices in a mesh: grp: 2 (over y), pol: 16 (over z, x, core).
Axes of the slice: x: 2, y: 2, z: 4, core: 2. Of those that a mesh axis runs over, the one named last changes fastest.
Arguments:
- shocks: float32 [6, 128, 1024], P('grp'), parts along dimension 0, may hold values from -6 to 6
- loadings: float32 [1024, 128], P('pol'), may hold values from -0.5 to 0.5
- sec_drift: float32 [1024], P('pol'), may hold values from -0.02 to 0.08
- holdings: float32 [1024, 128], P('pol'), may hold values from -0.1875 to 0.1875
- fund_of: int32 [8192, 1], P('pol'), may hold values from 0 to 127
- product_type: int32 [8192], P('pol'), may hold values from 0 to 7
- term_years: int32 [8192], P('pol'), may hold values from 1 to 3
- asset_start: float32 [8192], P('pol'), may hold values from 0.35 to 3
- liab_start: float32 [8192], P('pol'), may hold values from 0.3 to 3
- base_lapse: float32 [8], replicated, may hold values from 0.02 to 0.2
- guarantee: float32 [8], replicated, may hold values from 0 to 0.08
- lapse_draw: bfloat16 [8192, 6, 1024], P('pol', 'grp'), parts along dimension 1, may hold values from 0 to 1
Outputs:
- assets: float32 [8192, 2048], P('pol', 'grp'), parts along dimension 1
- liability: float32 [8192, 2048], P('pol', 'grp'), parts along dimension 1
- credit_rates: float32 [6, 128, 1024], P('grp', None, 'pol'), parts along dimension 0
The draws below stay inside these ranges and needn't reach their ends.
There are 2 independent parts, one for each index of `grp`. The reference program is written for one: setup_inputs(seed, part) draws one part's arguments, and reference() takes and returns one part's arrays. A program takes and returns all parts, laid end to end along the dimension named above; an argument that names none is the same for every part. Nothing has to cross between parts.
Inputs may be any that keep to these rules, and one draw needn't show every extreme that they name: `fund_of`: every fund backs at least one policy.
All inputs are finite; a program needn't handle non-finite values.
Results may differ from the reference program's by a relative error of at most 0.0003.
Values sent between devices are 32-bit elements; how exact they have to be, the bound alone decides.
No kernel may reach another device: no remote copies, remote signals or barrier semaphores. Data moves between devices by JAX's collectives and lax.ppermute only.
A program may use at most 64 MiB of HBM per device.

```python
import math
import jax
import jax.numpy as jnp
from jax import lax

F = 128
K = 128
P_SIZE = 1024
Y = 3
NT = 8
SECURITIES = 1024
POLICIES = 8192


def draw_term_years(key, part):
    picked = jax.random.randint(key, (POLICIES,), 0, 20, dtype=jnp.int32)
    years = jnp.where(picked < Y - 1, picked + 1, Y).astype(jnp.int32)
    position = jnp.arange(POLICIES, dtype=jnp.int32)
    years = jnp.where(position < Y - 1, position + 1, years)
    return years.astype(jnp.int32)


def with_ends(drawn, key, least, top_value):
    longest = drawn.shape.index(max(drawn.shape))
    spots = []
    for shift in (0, 1):
        where = [jax.random.randint(jax.random.fold_in(key, axis), (), 0, length) for axis, length in enumerate(drawn.shape)]
        where[longest] = (where[longest] + shift) % drawn.shape[longest]
        spots.append(tuple(where))
    return drawn.at[spots[0]].set(least).at[spots[1]].set(top_value)


def steps_of(rng, extent, cuts, smallest, high):
    def one(axis_at, parts):
        heights = jax.random.uniform(jax.random.fold_in(jax.random.fold_in(rng, 6), axis_at), (parts,), jnp.float32, smallest / len(cuts), high / len(cuts))
        return jnp.repeat(jnp.exp(heights), extent[axis_at] // parts).reshape((-1,) + (1,) * (len(extent) - axis_at - 1))

    level = one(*cuts[0])
    for cut in cuts[1:]:
        level = level * one(*cut)
    return level


def choose_distinct(key, rows, count, top, lift):
    sequence = jax.random.permutation(jax.random.fold_in(key, 1), count)
    favour = sequence
    for power in range(3):
        favour = favour * favour // count
    favour = favour * lift // count
    lots = jax.random.randint(jax.random.fold_in(key, 2), (rows, count), 0, 4096) + favour
    sure = jax.random.permutation(jax.random.fold_in(key, 3), rows)[jnp.arange(count) % rows]
    lots = jnp.where(jnp.arange(rows)[:, None] == sure[None, :], 1 << 14, lots)
    priority = lots * count + jnp.arange(count)
    return lax.top_k(priority.astype(jnp.int32), top)[1].astype(jnp.int32)


def noise(stream_key, dims, deviation, reach, cuts=(), kind=jnp.bfloat16):
    entries = deviation * jax.random.normal(stream_key, dims, jnp.float32)
    if cuts:
        entries = entries * steps_of(stream_key, dims, cuts, -0.22, 0.18)
    return jnp.clip(entries, -reach, reach).astype(kind)


def setup_inputs(seed: int = 0, part: int = 0) -> dict:
    splits = jax.random.split(jax.random.key(seed), 13)
    own_keys = jax.random.split(jax.random.fold_in(splits[12], part), 13)
    return {
        "shocks": noise(own_keys[0], (Y, K, P_SIZE), 1.0, 6.0, (), jnp.float32),
        "loadings": noise(splits[1], (SECURITIES, K), K ** -0.5, 0.5, ((0, 16),), jnp.float32),
        "sec_drift": jnp.clip(-0.02 + 0.09999999776482582 * jax.random.uniform(splits[2], (SECURITIES,), jnp.float32) ** steps_of(splits[2], (SECURITIES,), ((0, 16),), -0.2, 0.2), -0.02, 0.08),
        "holdings": noise(splits[3], (SECURITIES, F), SECURITIES ** -0.5, 0.1875, ((0, 16),), jnp.float32),
        "fund_of": choose_distinct(splits[4], POLICIES, F, 1, 0),
        "product_type": with_ends(jax.random.randint(splits[5], (POLICIES,), 0, NT), jax.random.fold_in(splits[5], 1), 0, NT - 1).astype(jnp.int32),
        "term_years": draw_term_years(jax.random.fold_in(splits[12], 71), part),
        "asset_start": jnp.clip(jnp.exp(math.log(3.0) - 2.1484344 * jax.random.uniform(splits[7], (POLICIES,), jnp.float32) ** steps_of(splits[7], (POLICIES,), ((0, 16),), -0.2, 0.2)), 0.35, 3.0),
        "liab_start": jnp.clip(jnp.exp(math.log(3.0) - 2.3025851 * jax.random.uniform(splits[8], (POLICIES,), jnp.float32) ** steps_of(splits[8], (POLICIES,), ((0, 16),), -0.2, 0.2)), 0.3, 3.0),
        "base_lapse": jnp.clip(jnp.exp(jax.random.uniform(splits[9], (NT,), jnp.float32, math.log(0.02), math.log(0.2))), 0.02, 0.2),
        "guarantee": jnp.clip(jax.random.uniform(splits[10], (NT,), jnp.float32, 0.0, 0.08), 0.0, 0.08),
        "lapse_draw": jnp.clip(1.0 * jax.random.uniform(own_keys[11], (POLICIES, Y, P_SIZE), jnp.float32) ** steps_of(own_keys[11], (POLICIES, Y, P_SIZE), ((0, 16),), -0.2, 0.2), 0.0, 1.0).astype(jnp.bfloat16),
    }


def reference(shocks, loadings, sec_drift, holdings, fund_of, product_type, term_years, asset_start, liab_start, base_lapse, guarantee, lapse_draw):
    highest = lax.Precision.HIGHEST
    sec_ret = 0.25 * jnp.tanh(jnp.einsum('sk,ykp->ysp', loadings, shocks, precision=highest)) + sec_drift[None, :, None]
    fund_ret = jnp.einsum('sf,ysp->yfp', holdings, sec_ret, precision=highest)
    fund_index = fund_of[:, 0]
    guaranteed = guarantee[product_type]
    base_rate = base_lapse[product_type]
    count = asset_start.shape[0]
    assets = jnp.broadcast_to(asset_start[:, None], (count, P_SIZE))
    liability = jnp.broadcast_to(liab_start[:, None], (count, P_SIZE))
    collected = []
    for year in range(Y):
        in_force = (term_years > year).astype(jnp.float32)[:, None]
        growth = fund_ret[year][fund_index]
        assets = assets * (1.0 + in_force * growth)
        asset_sums = jax.ops.segment_sum(in_force * assets, fund_index, num_segments=F)
        liab_sums = jax.ops.segment_sum(liability, fund_index, num_segments=F)
        declared = 0.01 + jax.nn.softplus(20.0 * (asset_sums / liab_sums - 1.05)) / 20.0
        credit = jnp.maximum(declared[fund_index], guaranteed[:, None])
        lapse_rate = jnp.minimum(base_rate[:, None] * (0.5 + lapse_draw[:, year, :].astype(jnp.float32)) * jnp.exp(5.0 * (growth - credit)), 0.5)
        liability = liability * (1.0 + in_force * credit) * (1.0 - in_force * lapse_rate)
        assets = assets * (1.0 - in_force * lapse_rate)
        collected.append(declared)
    return assets, liability, jnp.stack(collected)
```

```python
import jax
import jax.numpy as jnp
from jax import lax
from jax.sharding import PartitionSpec as P

HIGHEST = lax.Precision.HIGHEST
HIGH = lax.Precision.HIGH
SQUARE = (2, 4, 6)


def swap(x, offset):
    n = lax.axis_size("pol")
    return lax.ppermute(x, "pol", [(i, i ^ offset) for i in range(n)])


def far_offsets():
    n = lax.axis_size("pol")
    return [1 << b for b in range(3, n.bit_length() - 1)]


def reduce_slices(sums):
    held = sums[0] + swap(sums[1], 1)
    arrived = [swap(held[i + 1], o) for i, o in enumerate(SQUARE)]
    total = held[0] + arrived[0] + arrived[1] + arrived[2]
    for o in far_offsets():
        total = total + swap(total, o)
    return total


def gather_slices(own):
    near = jnp.stack([own] + [swap(own, o) for o in SQUARE])
    return jnp.concatenate([near, swap(near, 1)])


def rate(ratio):
    return 0.01 + jax.nn.softplus(20.0 * (ratio - 1.05)) / 20.0


def local(
    shocks,
    loadings,
    sec_drift,
    holdings,
    fund_of,
    product_type,
    term_years,
    asset_start,
    liab_start,
    base_lapse,
    guarantee,
    lapse_draw,
):
    num_years, _, num_paths = shocks.shape
    num_funds = holdings.shape[1]
    n = lax.axis_size("pol")
    me = lax.axis_index("pol")
    slice_funds = num_funds // 8
    count = asset_start.shape[0]
    funds = jnp.arange(num_funds, dtype=jnp.int32)
    member = (fund_of == funds[None, :]).astype(jnp.float32)
    offset = (fund_of // slice_funds) ^ (me & 7)
    place = ((offset & 1) * 4 + (offset >> 1)) * slice_funds + fund_of % slice_funds
    placed = (place == funds[None, :]).astype(jnp.float32)
    type_hot = (
        product_type[:, None] == jnp.arange(base_lapse.shape[0], dtype=jnp.int32)[None, :]
    ).astype(jnp.float32)
    guaranteed = jnp.sum(type_hot * guarantee[None, :], axis=1)
    base_rate = jnp.sum(type_hot * base_lapse[None, :], axis=1)
    in_force = [(term_years > year).astype(jnp.float32) for year in range(num_years)]

    start = jnp.stack([in_force[0] * asset_start, liab_start])
    start_sums = jnp.dot(start, member, precision=HIGHEST)
    secs = loadings.shape[0]
    drift_row = jnp.pad(sec_drift, (0, num_funds - secs))[None, :]
    extra = jnp.concatenate([start_sums, drift_row, jnp.zeros((5, num_funds), jnp.float32)])
    block = jnp.concatenate([loadings, holdings, extra])[None]
    for o in reversed(far_offsets()):
        block = jnp.concatenate([block, swap(block, o)])
    block = jnp.concatenate([block] + [swap(block, o) for o in SQUARE])
    all_load = block[:, :secs].reshape(-1, loadings.shape[1])
    all_hold = block[:, secs : 2 * secs].reshape(-1, num_funds)
    all_drift = block[:, 2 * secs + 2, :secs].reshape(-1)
    start_sums = jnp.sum(block[:, 2 * secs : 2 * secs + 2], axis=0)
    start_sums = start_sums + swap(start_sums, 1)

    def returns(year):
        sec = jnp.dot(all_load, shocks[year], precision=HIGH)
        sec = 0.25 * jnp.tanh(sec) + all_drift[:, None]
        part = lax.dot_general(all_hold, sec, (((0,), (0,)), ((), ())), precision=HIGH)
        return part + swap(part, 1)

    fund_ret = [returns(year) for year in range(num_years)]

    owned_paths = num_paths // n
    collected = []
    order = jnp.arange(8, dtype=jnp.int32) ^ (me & 7)
    order = (order & 1) * 4 + (order >> 1)
    assets, liability = asset_start[:, None], liab_start[:, None]
    for year in range(num_years):
        if year == 0:
            declared = rate(
                start_sums[0][:, None] * (1.0 + fund_ret[0]) / start_sums[1][:, None]
            )
            canonical, credit = declared, jnp.dot(member, declared, precision=HIGH)
        else:
            here = lax.dynamic_slice_in_dim(
                fund_ret[year], (me & 7) * slice_funds, slice_funds, 0
            )
            own = rate(totals[0] * (1.0 + here) / totals[1])
            declared = gather_slices(own)
            canonical = declared[order].reshape(num_funds, num_paths)
            credit = jnp.dot(placed, declared.reshape(num_funds, num_paths), precision=HIGH)
        collected.append(
            lax.dynamic_slice_in_dim(canonical, me * owned_paths, owned_paths, 1)
        )
        alive = in_force[year][:, None]
        growth = jnp.dot(member, fund_ret[year], precision=HIGH)
        credit = jnp.maximum(credit, guaranteed[:, None])
        lapse_rate = jnp.minimum(
            base_rate[:, None]
            * (0.5 + lapse_draw[:, year, :].astype(jnp.float32))
            * jnp.exp(5.0 * (growth - credit)),
            0.5,
        )
        stay = 1.0 - alive * lapse_rate
        assets = assets * (1.0 + alive * growth) * stay
        liability = liability * (1.0 + alive * credit) * stay
        if year + 1 < num_years:
            sums = jnp.stack(
                [
                    jnp.dot(placed.T, in_force[year + 1][:, None] * assets, precision=HIGH),
                    jnp.dot(placed.T, liability, precision=HIGH),
                ]
            ).reshape(2, 2, 4, slice_funds, num_paths)
            totals = reduce_slices(sums.transpose(1, 2, 0, 3, 4))
    return (assets, liability, jnp.stack(collected))


def solution(mesh):
    in_specs = (
        P("grp", None, None),
        P("pol", None),
        P("pol"),
        P("pol", None),
        P("pol", None),
        P("pol"),
        P("pol"),
        P("pol"),
        P("pol"),
        P(),
        P(),
        P("pol", "grp", None),
    )
    out_specs = (P("pol", "grp"), P("pol", "grp"), P("grp", None, "pol"))
    return jax.shard_map(local, mesh=mesh, in_specs=in_specs, out_specs=out_specs, check_vma=False)
```

```python
import functools

import jax
import jax.numpy as jnp
from jax import lax
from jax.experimental import pallas as pl
from jax.experimental.pallas import tpu as pltpu
from jax.sharding import PartitionSpec as P

F32, BF16 = jnp.float32, jnp.bfloat16
SQUARE = (2, 4, 6)
VMEM = pl.BlockSpec(memory_space=pltpu.VMEM)
SMEM = pl.BlockSpec(memory_space=pltpu.SMEM)
ANY = pl.BlockSpec(memory_space=pl.ANY)
ROW = (((1,), (1,)), ((), ()))


def swap(x, offset):
    n = lax.axis_size("pol")
    return lax.ppermute(x, "pol", [(i, i ^ offset) for i in range(n)])


def far_offsets():
    n = lax.axis_size("pol")
    return [1 << b for b in range(3, n.bit_length() - 1)]


def rate(ratio):
    x = 20.0 * (ratio - 1.05)
    return 0.01 + (jnp.maximum(x, 0.0) + jnp.log1p(jnp.exp(-jnp.abs(x)))) / 20.0


def halves(v):
    hi = v.astype(BF16)
    return hi, (v - hi.astype(F32)).astype(BF16)


def dot(a, b, dims=(((1,), (0,)), ((), ()))):
    return lax.dot_general(a, b, dims, preferred_element_type=F32)


def call(body, out, ins, name, flops=0, moved=0, scratch=(), out_specs=None, limit=24):
    return pl.pallas_call(
        body,
        out_shape=out,
        in_specs=ins,
        out_specs=out_specs if out_specs is not None else jax.tree.map(lambda _: VMEM, out),
        scratch_shapes=scratch,
        compiler_params=pltpu.CompilerParams(vmem_limit_bytes=limit << 20),
        cost_estimate=pl.CostEstimate(flops=flops, bytes_accessed=moved, transcendentals=0),
        name=name,
    )


def shaped(*dims, dtype=F32):
    return jax.ShapeDtypeStruct(dims, dtype)


def pack_body(load, hold, drift, fund, term, asset, liab, out):
    secs, funds = load.shape
    count = fund.shape[1]
    out[0:secs, :] = load[...]
    out[secs : 2 * secs, :] = hold[...]
    member = (lax.broadcasted_iota(jnp.int32, (funds, count), 0) == fund[...]).astype(BF16)
    at = lax.broadcasted_iota(jnp.int32, (8, count), 0)
    alive = (term[...] > 0).astype(F32)
    v = jnp.where(at < 3, asset[...] * alive, liab[...])
    one, rest = v.astype(BF16).astype(F32), v - v.astype(BF16).astype(F32)
    two = rest.astype(BF16).astype(F32)
    three = rest - two
    kind = jnp.where(at < 3, at, at - 3)
    rows = jnp.where(kind == 0, one, jnp.where(kind == 1, two, three))
    rows = jnp.where(at < 6, rows, 0.0).astype(BF16)
    out[2 * secs : 2 * secs + 8, :] = dot(rows, member, ROW)
    out[2 * secs + 6 : 2 * secs + 7, 0:secs] = drift[...]


def columns_body(base, guar, fund, kind, term, asset, liab, *outs):
    years = (len(outs) - 2) // 4
    member_t, member, base_w, guar_w = (outs[i * years : (i + 1) * years] for i in range(4))
    asset_w, liab_w = outs[-2:]
    funds, count = member_t[0].shape
    types = base.shape[0]
    base_row = jnp.zeros((1, count), F32)
    guar_row = jnp.zeros((1, count), F32)
    for t in range(types):
        base_row = jnp.where(kind[...] == t, base[t], base_row)
        guar_row = jnp.where(kind[...] == t, guar[t], guar_row)
    at = lax.broadcasted_iota(jnp.int32, (128, count), 0)
    rows = (fund[...].astype(F32), term[...].astype(F32), base_row, guar_row, asset[...], liab[...])
    stack = jnp.zeros((128, count), F32)
    for r, row in enumerate(rows):
        stack = jnp.where(at == r, row, stack)
    cols = jnp.transpose(stack)
    wide = lambda r: jnp.broadcast_to(cols[:, r : r + 1], (count, 128))
    fund_c, term_c, base_c, guar_c = wide(0), wide(1), wide(2), wide(3)
    asset_w[...] = wide(4)
    liab_w[...] = wide(5)
    hot_t = lax.broadcasted_iota(jnp.int32, (funds, count), 0) == fund[...]
    hot = lax.broadcasted_iota(jnp.int32, (count, funds), 1).astype(F32) == fund_c
    for y in range(years):
        alive = term_c > float(y)
        base_w[y][...] = jnp.where(alive, base_c, 0.0)
        guar_w[y][...] = jnp.where(alive, guar_c, 0.0)
        here = jnp.logical_and(hot, alive).astype(F32).astype(BF16)
        member[y][:, 0:funds] = here
        member[y][:, funds : 2 * funds] = here
        if y == 0:
            member_t[y][...] = hot_t.astype(F32).astype(BF16)
        else:
            member_t[y][...] = jnp.logical_and(hot_t, term[...] > y).astype(F32).astype(BF16)


def returns_body(year, first, secs, *refs):
    blocks, (shocks, part, sums), (load_hi, load_lo, hold_hi, hold_lo) = refs[:4], refs[4:7], refs[7:]
    funds, width = part.shape
    total = load_hi.shape[0]
    at = 0
    extra = jnp.zeros((8, funds), F32)
    fixed = jnp.zeros((8, funds), F32)
    for block in blocks:
        for b in range(block.shape[0]):
            load_hi[at : at + secs, :], load_lo[at : at + secs, :] = halves(block[b, 0:secs, :])
            hold = block[b, secs : 2 * secs, :]
            hold_hi[at : at + secs, :], hold_lo[at : at + secs, :] = halves(hold)
            tail = block[b, 2 * secs : 2 * secs + 8, :]
            extra = extra + tail
            fixed = fixed + jnp.dot(tail[:, 0:secs], hold, precision=lax.Precision.HIGHEST)
            at += secs
    sums[...] = extra
    row = lax.broadcasted_iota(jnp.int32, (128, funds), 0)
    fixed_col = jnp.transpose(jnp.where(row == 0, fixed[6:7, :], 0.0))[:, 0:1]
    step = min(256, width)
    group = min(512, total)
    for c in range(0, width, step):
        x_hi, x_lo = halves(shocks[year, :, first + c : first + c + step])
        acc = jnp.zeros((funds, step), F32)
        for g in range(0, total, group):
            lh, ll = load_hi[g : g + group, :], load_lo[g : g + group, :]
            z = dot(jnp.concatenate([lh, lh], 1), jnp.concatenate([x_hi, x_lo], 0)) + dot(ll, x_hi)
            t_hi, t_lo = halves(jnp.tanh(z))
            hh, hl = hold_hi[g : g + group, :], hold_lo[g : g + group, :]
            over = (((0,), (0,)), ((), ()))
            acc = acc + dot(hh, t_hi, over) + dot(hh, t_lo, over) + dot(hl, t_hi, over)
        part[:, c : c + step] = 0.25 * acc + fixed_col


def own_columns(me_ref, declared, first, out):
    paths, funds = out.shape
    width = declared.shape[1]
    spot = lax.broadcasted_iota(jnp.int32, (paths, width), 1) + first
    pick = spot == lax.broadcasted_iota(jnp.int32, (paths, width), 0) + me_ref[0] * paths
    pick = pick.astype(F32).astype(BF16)
    one, rest = declared.astype(BF16), declared - declared.astype(BF16).astype(F32)
    two, three = halves(rest)
    out[...] = dot(pick, one, ROW) + dot(pick, two, ROW) + dot(pick, three, ROW)


def slice_spot(me_ref, order, slice_funds):
    label = (order >> 2) | ((order & 3) << 1)
    return pl.multiple_of(((me_ref[0] & 7) ^ label) * slice_funds, slice_funds)


def advance(cols, c, step, table, member, base, guar, draw, asset, liab):
    wide = lambda v: jnp.concatenate([v] * (step // 128), 1)
    got = dot(member, table)
    growth, credit = got[:, 0:step], jnp.maximum(got[:, step:], wide(guar))
    lapse = jnp.minimum(wide(base) * (0.5 + draw.astype(F32)) * jnp.exp(5.0 * (growth - credit)), 0.5)
    stay = 1.0 - lapse
    return asset * (1.0 + growth) * stay, liab * (1.0 + credit) * stay


def table_of(growth, declared):
    g_hi, g_lo = halves(growth)
    d_hi, d_lo = halves(declared)
    return jnp.concatenate([jnp.concatenate([g_hi, d_hi], 1), jnp.concatenate([g_lo, d_lo], 1)], 0)


STEP, ROWS = 256, 256


def year_body(year, first, last, slice_funds, *refs):
    refs = list(refs)
    me = refs.pop(0)
    if year == 0:
        mine, other = refs.pop(0), refs.pop(0)
    else:
        near, far = refs.pop(0), refs.pop(0)
    part, peer = refs.pop(0), refs.pop(0)
    draws, member, base, guar = (refs.pop(0) for _ in range(4))
    states = [(refs.pop(0), refs.pop(0)) for _ in range(2 if last else 1)]
    if last:
        earlier = [refs.pop(0) for _ in range(2 * year)]
        out_a, out_l, out_r, declared, buf_a, buf_l, sem = refs
    else:
        member_t, member_ta = refs.pop(0), refs.pop(0)
        out_a, out_l, out_s, out_r, declared, acc = refs
    funds, width = declared.shape
    count = member.shape[0]
    if year == 0:
        sums = mine[...] + other[...]
        row = lax.broadcasted_iota(jnp.int32, (128, funds), 0)
        start_a = sums[0:1, :] + sums[1:2, :] + sums[2:3, :]
        start_l = sums[3:4, :] + sums[4:5, :] + sums[5:6, :]
        both = jnp.where(row == 0, start_a, jnp.where(row == 1, start_l, 0.0))
        both = jnp.transpose(both)
        ratio = both[:, 0:1] / both[:, 1:2]
        declared[...] = rate(ratio * (1.0 + (part[...] + peer[...])))
    else:
        for o in range(8):
            source = near if o < 4 else far
            declared[pl.ds(slice_spot(me, o, slice_funds), slice_funds), :] = source[
                o & 3, :, first : first + width
            ]
    if last:
        own = out_r.at[year]
        for y in range(year):
            out_r[y] = earlier[2 * y][...] + earlier[2 * y + 1][...]
    else:
        own = out_r
    copies = []
    for c in range(0, width, STEP):
        cut = slice(c, c + STEP)
        table = table_of(part[:, cut] + peer[:, cut], declared[:, cut])
        sum_a = sum_l = None
        for r in range(0, count, ROWS):
            rows = slice(r, r + ROWS)
            if year == 0:
                asset = jnp.concatenate([states[0][0][rows, :]] * (STEP // 128), 1)
                liab = jnp.concatenate([states[0][1][rows, :]] * (STEP // 128), 1)
            else:
                half = states[0][0].shape[1]
                held = states[c // half]
                at = slice(c % half, c % half + STEP)
                asset, liab = held[0][rows, at], held[1][rows, at]
            asset, liab = advance(
                None, c, STEP, table, member[rows, :], base[rows, :], guar[rows, :],
                draws[year, rows, first + c : first + c + STEP], asset, liab,
            )
            if last:
                buf_a[c // STEP, rows, :] = asset
                buf_l[c // STEP, rows, :] = liab
            else:
                out_a[rows, cut] = asset
                out_l[rows, cut] = liab
                a_hi, a_lo = halves(asset)
                l_hi, l_lo = halves(liab)
                ma, ml = member_ta[:, rows], member_t[:, rows]
                add_a = dot(ma, a_hi) + dot(ma, a_lo)
                add_l = dot(ml, l_hi) + dot(ml, l_lo)
                sum_a = add_a if sum_a is None else sum_a + add_a
                sum_l = add_l if sum_l is None else sum_l + add_l
        if last:
            for buf, out, k in ((buf_a, out_a, 0), (buf_l, out_l, 1)):
                copy = pltpu.make_async_copy(buf.at[c // STEP], out.at[:, cut], sem.at[k, c // STEP])
                copy.start()
                copies.append(copy)
        else:
            acc[0, :, cut] = sum_a
            acc[1, :, cut] = sum_l
    own_columns(me, declared[...], first, own)
    if last:
        for copy in copies:
            copy.wait()
    else:
        for o in range(8):
            for v in range(2):
                out_s[o // 4, o % 4, v] = acc[v, pl.ds(slice_spot(me, o, slice_funds), slice_funds), :]


def local(
    shocks,
    loadings,
    sec_drift,
    holdings,
    fund_of,
    product_type,
    term_years,
    asset_start,
    liab_start,
    base_lapse,
    guarantee,
    lapse_draw,
):
    years, _, paths = shocks.shape
    secs, funds = holdings.shape
    count = asset_start.shape[0]
    n = lax.axis_size("pol")
    me = lax.axis_index("pol")
    me_ref = me.astype(jnp.int32).reshape(1)
    slice_funds = funds // 8
    owned = paths // n
    half = paths // 2
    draws = lapse_draw.transpose(1, 0, 2)
    line = lambda v: v.reshape(1, count)
    fund, kind, term = line(fund_of), line(product_type), line(term_years)
    asset, liab = line(asset_start), line(liab_start)

    block = call(pack_body, shaped(2 * secs + 8, funds), [VMEM] * 7, "pack", 10**6, 10**5)(
        loadings, holdings, sec_drift.reshape(1, secs), fund, term, asset, liab
    )
    fund, kind, term, asset, liab, block = lax.optimization_barrier(
        (fund, kind, term, asset, liab, block)
    )
    block = block[None]
    for o in reversed(far_offsets()):
        block = jnp.concatenate([block, swap(block, o)])
    blocks = [block] + [swap(block, o) for o in SQUARE]

    wide = shaped(count, 128)
    made = call(
        columns_body,
        [shaped(funds, count, dtype=BF16)] * years
        + [shaped(count, 2 * funds, dtype=BF16)] * years
        + [wide] * (2 * years + 2),
        [SMEM] * 2 + [VMEM] * 5,
        "columns",
        10**6,
        4 * 10**6,
    )(base_lapse, guarantee, fund, kind, term, asset, liab)
    member_t, member, base_w, guar_w = (made[i * years : (i + 1) * years] for i in range(4))
    asset_w, liab_w = made[-2:]

    total = secs * n // 2

    def returns(year, first, width):
        part, sums = call(
            functools.partial(returns_body, year, first, secs),
            [shaped(funds, width), shaped(8, funds)],
            [VMEM] * 5,
            "returns",
            flops=2 * 6 * total * funds * width,
            moved=4 * funds * width,
            scratch=[pltpu.VMEM((total, funds), BF16)] * 4,
            limit=32,
        )(*blocks, shocks)
        return part, sums

    parts = [[returns(0, h * half, half) for h in range(2)]]
    sums = parts[0][0][1]
    parts[0] = [p for p, _ in parts[0]]
    parts += [[returns(y, 0, paths)[0]] for y in range(1, years)]
    peers = [[swap(p, 1) for p in ps] for ps in parts]
    other_sums = swap(sums, 1)

    state = [(asset_w, liab_w)] * 2
    rates = []
    for year in range(years):
        last = year + 1 == years
        if year == 0:
            head = [sums, other_sums]
        else:
            near = jnp.stack([own] + [swap(own, o) for o in SQUARE])
            head = [near, swap(near, 1)]
        shares = []
        for h in range(1 if last else 2):
            width = paths if last else half
            first = h * half
            if year == 0:
                pair = [parts[0][h], peers[0][h]]
            else:
                pair = [parts[year][0][:, first : first + width], peers[year][0][:, first : first + width]]
            ins = [me_ref] + head + pair + [draws, member[year], base_w[year], guar_w[year]]
            cost = dict(flops=2 * 2 * count * 2 * funds * width, moved=20 * count * width)
            if last:
                ins += [v for s in state for v in s] + [v for rs in rates for v in rs]
                out = [shaped(count, paths), shaped(count, paths), shaped(years, owned, funds)]
                out_specs = [ANY, ANY, VMEM]
                tiles = paths // STEP
                scratch = [pltpu.VMEM((funds, width), F32)]
                scratch += [pltpu.VMEM((tiles, count, STEP), F32)] * 2
                scratch += [pltpu.SemaphoreType.DMA((2, tiles))]
            else:
                ins += list(state[h]) + [member_t[0], member_t[year + 1]]
                out = [shaped(count, width)] * 2
                out += [shaped(2, 4, 2, slice_funds, width), shaped(owned, funds)]
                out_specs = None
                scratch = [pltpu.VMEM((funds, width), F32), pltpu.VMEM((2, funds, width), F32)]
            shares.append(
                call(
                    functools.partial(year_body, year, first, last, slice_funds),
                    out,
                    [SMEM] + [VMEM] * (len(ins) - 1),
                    "year",
                    scratch=scratch,
                    out_specs=out_specs,
                    limit=32,
                    **cost,
                )(*ins)
            )
        if last:
            assets, liability, credit = shares[0]
            return assets, liability, credit.transpose(0, 2, 1)
        state = [(s[0], s[1]) for s in shares]
        rates.append([s[3] for s in shares])
        held = jnp.concatenate([s[2][0] + swap(s[2][1], 1) for s in shares], -1)
        arrived = [swap(held[i + 1], o) for i, o in enumerate(SQUARE)]
        totals = held[0] + arrived[0] + arrived[1] + arrived[2]
        for o in far_offsets():
            totals = totals + swap(totals, o)
        here = lax.dynamic_slice_in_dim(
            parts[year + 1][0], (me & 7) * slice_funds, slice_funds, 0
        ) + lax.dynamic_slice_in_dim(
            peers[year + 1][0], (me & 7) * slice_funds, slice_funds, 0
        )
        own = rate(totals[0] * (1.0 + here) / totals[1])


def solution(mesh):
    in_specs = (
        P("grp", None, None),
        P("pol", None),
        P("pol"),
        P("pol", None),
        P("pol", None),
        P("pol"),
        P("pol"),
        P("pol"),
        P("pol"),
        P(),
        P(),
        P("pol", "grp", None),
    )
    out_specs = (P("pol", "grp"), P("pol", "grp"), P("grp", None, "pol"))
    return jax.shard_map(local, mesh=mesh, in_specs=in_specs, out_specs=out_specs, check_vma=False)
```

```python
import functools

import jax
import jax.numpy as jnp
from jax import lax
from jax.experimental import pallas as pl
from jax.experimental.pallas import tpu as pltpu
from jax.sharding import PartitionSpec as P

F32, BF16 = jnp.float32, jnp.bfloat16
SQUARE = (2, 4, 6)
VMEM = pl.BlockSpec(memory_space=pltpu.VMEM)
SMEM = pl.BlockSpec(memory_space=pltpu.SMEM)
ANY = pl.BlockSpec(memory_space=pl.ANY)
HBM = pl.BlockSpec(memory_space=pltpu.HBM)
ROW = (((1,), (1,)), ((), ()))


def swap(x, offset):
    n = lax.axis_size("pol")
    return lax.ppermute(x, "pol", [(i, i ^ offset) for i in range(n)])


def far_offsets():
    n = lax.axis_size("pol")
    return [1 << b for b in range(3, n.bit_length() - 1)]


def rate(ratio):
    x = 20.0 * (ratio - 1.05)
    return 0.01 + (jnp.maximum(x, 0.0) + jnp.log1p(jnp.exp(-jnp.abs(x)))) / 20.0


def halves(v):
    hi = v.astype(BF16)
    return hi, (v - hi.astype(F32)).astype(BF16)


def dot(a, b, dims=(((1,), (0,)), ((), ()))):
    return lax.dot_general(a, b, dims, preferred_element_type=F32)


def call(body, out, ins, name, flops=0, moved=0, scratch=(), out_specs=None, limit=24):
    return pl.pallas_call(
        body,
        out_shape=out,
        in_specs=ins,
        out_specs=out_specs if out_specs is not None else jax.tree.map(lambda _: VMEM, out),
        scratch_shapes=scratch,
        compiler_params=pltpu.CompilerParams(vmem_limit_bytes=int(limit * 2**20)),
        cost_estimate=pl.CostEstimate(flops=flops, bytes_accessed=moved, transcendentals=0),
        name=name,
    )


def shaped(*dims, dtype=F32):
    return jax.ShapeDtypeStruct(dims, dtype)


def pack_body(*refs):
    sources, (out, lines), held, sem = refs[1:11], refs[11:13], refs[13:23], refs[23]
    copies = [pltpu.make_async_copy(s, h, sem.at[i]) for i, (s, h) in enumerate(zip(sources, held))]
    for copy in copies:
        copy.start()
    for copy in copies:
        copy.wait()
    load, hold, drift, fund, term, asset, liab, kind, base, guar = held
    secs, funds = load.shape
    count = fund.shape[1]
    out[0:secs, :] = load[...]
    out[secs : 2 * secs, :] = hold[...]
    member = (lax.broadcasted_iota(jnp.int32, (funds, count), 0) == fund[...]).astype(BF16)
    at = lax.broadcasted_iota(jnp.int32, (8, count), 0)
    alive = (term[...] > 0).astype(F32)
    v = jnp.where(at < 3, asset[...] * alive, liab[...])
    one, rest = v.astype(BF16).astype(F32), v - v.astype(BF16).astype(F32)
    two = rest.astype(BF16).astype(F32)
    three = rest - two
    spot = jnp.where(at < 3, at, at - 3)
    rows = jnp.where(spot == 0, one, jnp.where(spot == 1, two, three))
    rows = jnp.where(at < 6, rows, 0.0).astype(BF16)
    out[2 * secs : 2 * secs + 8, :] = dot(rows, member, ROW)
    out[2 * secs + 6 : 2 * secs + 7, 0:secs] = drift[...]
    base_row = jnp.zeros((1, count), F32)
    guar_row = jnp.zeros((1, count), F32)
    for t in range(base.shape[1]):
        base_row = jnp.where(kind[...] == t, base[:, t : t + 1], base_row)
        guar_row = jnp.where(kind[...] == t, guar[:, t : t + 1], guar_row)
    values = (fund[...].astype(F32), term[...].astype(F32), base_row, guar_row, asset[...], liab[...])
    stack = jnp.zeros((8, count), F32)
    for r, row in enumerate(values):
        stack = jnp.where(at == r, row, stack)
    lines[...] = stack


def columns_body(lines, block, shocks, member_t, member, wides, x_now, x_later, own, raw, sem):
    own[0] = block[...]
    years, funds, count = member_t.shape
    fetch = pltpu.make_async_copy(shocks, raw, sem)
    fetch.start()
    stack = jnp.concatenate([lines[...], jnp.zeros((120, count), F32)], 0)
    cols = jnp.transpose(stack)
    wide = lambda r: jnp.broadcast_to(cols[:, r : r + 1], (count, 128))
    fund_c, term_c, base_c, guar_c = wide(0), wide(1), wide(2), wide(3)
    wides[2 * years] = wide(4)
    wides[2 * years + 1] = wide(5)
    hot_t = lax.broadcasted_iota(jnp.int32, (funds, count), 0).astype(F32) == lines[0:1, :]
    hot = lax.broadcasted_iota(jnp.int32, (count, funds), 1).astype(F32) == fund_c
    for y in range(years):
        alive = term_c > float(y)
        wides[2 * y] = jnp.where(alive, base_c, 0.0)
        wides[2 * y + 1] = jnp.where(alive, guar_c, 0.0)
        here = jnp.logical_and(hot, alive).astype(F32).astype(BF16)
        member[y, :, 0:funds] = here
        member[y, :, funds : 2 * funds] = here
        if y == 0:
            member_t[y] = hot_t.astype(F32).astype(BF16)
        else:
            member_t[y] = jnp.logical_and(hot_t, lines[1:2, :] > float(y)).astype(F32).astype(BF16)
    fetch.wait()
    for y in range(years):
        hi, lo = halves(raw[y])
        if y == 0:
            x_now[0], x_now[1] = hi, lo
        else:
            x_later[y - 1, 0], x_later[y - 1, 1] = hi, lo


def returns_body(year, first, secs, *refs):
    blocks, (xs, part, sums), (load_hi, load_lo, hold_hi, hold_lo) = refs[:4], refs[4:7], refs[7:]
    funds, width = part.shape
    total = load_hi.shape[0]
    at = 0
    extra = jnp.zeros((8, funds), F32)
    fixed = jnp.zeros((8, funds), F32)
    for block in blocks:
        for b in range(block.shape[0]):
            load_hi[at : at + secs, :], load_lo[at : at + secs, :] = halves(block[b, 0:secs, :])
            hold = block[b, secs : 2 * secs, :]
            hold_hi[at : at + secs, :], hold_lo[at : at + secs, :] = halves(hold)
            tail = block[b, 2 * secs : 2 * secs + 8, :]
            extra = extra + tail
            fixed = fixed + jnp.dot(tail[:, 0:secs], hold, precision=lax.Precision.HIGHEST)
            at += secs
    sums[...] = extra
    row = lax.broadcasted_iota(jnp.int32, (128, funds), 0)
    fixed_col = jnp.transpose(jnp.where(row == 0, fixed[6:7, :], 0.0))[:, 0:1]
    step = min(256, width)
    group = min(512, total)
    for c in range(0, width, step):
        cut = slice(first + c, first + c + step)
        x_hi, x_lo = (xs[i, :, cut] if year == 0 else xs[year - 1, i, :, cut] for i in range(2))
        acc = jnp.zeros((funds, step), F32)
        for g in range(0, total, group):
            lh, ll = load_hi[g : g + group, :], load_lo[g : g + group, :]
            z = dot(jnp.concatenate([lh, lh], 1), jnp.concatenate([x_hi, x_lo], 0)) + dot(ll, x_hi)
            t_hi, t_lo = halves(jnp.tanh(z))
            hh, hl = hold_hi[g : g + group, :], hold_lo[g : g + group, :]
            over = (((0,), (0,)), ((), ()))
            acc = acc + dot(hh, t_hi, over) + dot(hh, t_lo, over) + dot(hl, t_hi, over)
        part[:, c : c + step] = 0.25 * acc + fixed_col


def own_columns(me_ref, declared, first, out):
    paths, funds = out.shape
    width = declared.shape[1]
    spot = lax.broadcasted_iota(jnp.int32, (paths, width), 1) + first
    pick = spot == lax.broadcasted_iota(jnp.int32, (paths, width), 0) + me_ref[0] * paths
    pick = pick.astype(F32).astype(BF16)
    one, rest = declared.astype(BF16), declared - declared.astype(BF16).astype(F32)
    two, three = halves(rest)
    out[...] = dot(pick, one, ROW) + dot(pick, two, ROW) + dot(pick, three, ROW)


def slice_spot(me_ref, order, slice_funds):
    label = (order >> 2) | ((order & 3) << 1)
    return pl.multiple_of(((me_ref[0] & 7) ^ label) * slice_funds, slice_funds)


def advance(step, table, member, base, guar, draw, asset, liab):
    wide = lambda v: jnp.concatenate([v] * (step // 128), 1)
    got = dot(member, table)
    growth, credit = got[:, 0:step], jnp.maximum(got[:, step:], wide(guar))
    lapse = jnp.minimum(wide(base) * (0.5 + draw.astype(F32)) * jnp.exp(5.0 * (growth - credit)), 0.5)
    stay = 1.0 - lapse
    return asset * (1.0 + growth) * stay, liab * (1.0 + credit) * stay


def table_of(growth, declared):
    g_hi, g_lo = halves(growth)
    d_hi, d_lo = halves(declared)
    return jnp.concatenate([jnp.concatenate([g_hi, d_hi], 1), jnp.concatenate([g_lo, d_lo], 1)], 0)


def own_body(slice_funds, me, part, peer, *refs):
    totals, out = refs[:-1], refs[-1]
    rows = pl.ds(pl.multiple_of((me[0] & 7) * slice_funds, slice_funds), slice_funds)
    growth = part[rows, :] + peer[rows, :]
    asset, liab = totals[0][0], totals[0][1]
    for t in totals[1:]:
        asset, liab = asset + t[0], liab + t[1]
    out[...] = rate(asset * (1.0 + growth) / liab)


STEP, ROWS = 256, 256


def year_body(year, first, last, slice_funds, *refs):
    refs = list(refs)
    me = refs.pop(0)
    if year == 0:
        mine, other = refs.pop(0), refs.pop(0)
    else:
        slices = [refs.pop(0) for _ in range(8)]
    part, peer = refs.pop(0), refs.pop(0)
    draws, member, wides = refs.pop(0), refs.pop(0), refs.pop(0)
    states = [(refs.pop(0), refs.pop(0)) for _ in range(0 if year == 0 else 2 if last else 1)]
    lead = 0
    if last:
        earlier = [refs.pop(0) for _ in range(2 * year)]
        out_a, out_l, out_r, declared, buf_a, buf_l, sem = refs
    else:
        member_t = refs.pop(0)
        out_a, out_l, out_s, out_r, declared, acc = refs
    funds, width = declared.shape
    count = member.shape[1]
    if year == 0:
        sums = mine[...] + other[...]
        row = lax.broadcasted_iota(jnp.int32, (128, funds), 0)
        start_a = sums[0:1, :] + sums[1:2, :] + sums[2:3, :]
        start_l = sums[3:4, :] + sums[4:5, :] + sums[5:6, :]
        both = jnp.where(row == 0, start_a, jnp.where(row == 1, start_l, 0.0))
        both = jnp.transpose(both)
        ratio = both[:, 0:1] / both[:, 1:2]
        declared[...] = rate(ratio * (1.0 + (part[...] + peer[...])))
    else:
        lead = first
        for o in range(8):
            spot = pl.ds(slice_spot(me, o, slice_funds), slice_funds)
            declared[spot, :] = slices[o][:, first : first + width]
    if last:
        own = out_r.at[year]
        for y in range(year):
            out_r[y] = earlier[2 * y][...] + earlier[2 * y + 1][...]
    else:
        own = out_r
    copies = []
    for c in range(0, width, STEP):
        cut = slice(c, c + STEP)
        there = slice(lead + c, lead + c + STEP)
        table = table_of(part[:, there] + peer[:, there], declared[:, cut])
        sum_a = sum_l = None
        for r in range(0, count, ROWS):
            rows = slice(r, r + ROWS)
            if year == 0:
                years = member.shape[0]
                asset = jnp.concatenate([wides[2 * years, rows, :]] * (STEP // 128), 1)
                liab = jnp.concatenate([wides[2 * years + 1, rows, :]] * (STEP // 128), 1)
            else:
                half = states[0][0].shape[1]
                held = states[c // half]
                at = slice(c % half, c % half + STEP)
                asset, liab = held[0][rows, at], held[1][rows, at]
            asset, liab = advance(
                STEP, table, member[year, rows, :], wides[2 * year, rows, :], wides[2 * year + 1, rows, :],
                draws[year, rows, first + c : first + c + STEP], asset, liab,
            )
            if last:
                buf_a[c // STEP, rows, :] = asset
                buf_l[c // STEP, rows, :] = liab
            else:
                out_a[rows, cut] = asset
                out_l[rows, cut] = liab
                a_hi, a_lo = halves(asset)
                l_hi, l_lo = halves(liab)
                ma, ml = member_t[year + 1, :, rows], member_t[0, :, rows]
                add_a = dot(ma, a_hi) + dot(ma, a_lo)
                add_l = dot(ml, l_hi) + dot(ml, l_lo)
                sum_a = add_a if sum_a is None else sum_a + add_a
                sum_l = add_l if sum_l is None else sum_l + add_l
        if last:
            for buf, out, k in ((buf_a, out_a, 0), (buf_l, out_l, 1)):
                copy = pltpu.make_async_copy(buf.at[c // STEP], out.at[:, cut], sem.at[k, c // STEP])
                copy.start()
                copies.append(copy)
        else:
            acc[0, :, cut] = sum_a
            acc[1, :, cut] = sum_l
    own_columns(me, declared[...], first, own)
    if last:
        for copy in copies:
            copy.wait()
    else:
        for o in range(8):
            for v in range(2):
                out_s[o // 4, o % 4, v] = acc[v, pl.ds(slice_spot(me, o, slice_funds), slice_funds), :]


def local(
    shocks,
    loadings,
    sec_drift,
    holdings,
    fund_of,
    product_type,
    term_years,
    asset_start,
    liab_start,
    base_lapse,
    guarantee,
    lapse_draw,
):
    years, _, paths = shocks.shape
    secs, funds = holdings.shape
    count = asset_start.shape[0]
    n = lax.axis_size("pol")
    me = lax.axis_index("pol")
    me_ref = me.astype(jnp.int32).reshape(1)
    slice_funds = funds // 8
    owned = paths // n
    half = paths // 2
    draws = lapse_draw.transpose(1, 0, 2)
    line = lambda v: v.reshape(1, count)
    fund, kind, term = line(fund_of), line(product_type), line(term_years)
    asset, liab = line(asset_start), line(liab_start)

    sources = [loadings, holdings, sec_drift.reshape(1, secs), fund, term, asset, liab, kind]
    sources += [base_lapse.reshape(1, -1), guarantee.reshape(1, -1)]
    block, lines = call(
        pack_body,
        [shaped(2 * secs + 8, funds), shaped(8, count)],
        [SMEM] + [HBM] * 10,
        "pack",
        10**6,
        10**5,
        scratch=[pltpu.VMEM(v.shape, v.dtype) for v in sources] + [pltpu.SemaphoreType.DMA((10,))],
        limit=60,
    )(me_ref, *sources)
    far = far_offsets()
    came = swap(block[None], far[-1])
    member_t, member, wides, x_now, x_later, block = call(
        columns_body,
        [
            shaped(years, funds, count, dtype=BF16),
            shaped(years, count, 2 * funds, dtype=BF16),
            shaped(2 * years + 2, count, 128),
            shaped(2, *shocks.shape[1:], dtype=BF16),
            shaped(years - 1, 2, *shocks.shape[1:], dtype=BF16),
            shaped(1, *block.shape),
        ],
        [VMEM, VMEM, HBM],
        "columns",
        10**6,
        4 * 10**6,
        scratch=[pltpu.VMEM(shocks.shape, F32), pltpu.SemaphoreType.DMA],
        limit=8,
    )(lines, block, shocks)
    came, block = lax.optimization_barrier((came, block))
    block = jnp.concatenate([block, came])
    for o in reversed(far[:-1]):
        block = jnp.concatenate([block, swap(block, o)])
    blocks = [block] + [swap(block, o) for o in SQUARE]

    total = secs * n // 2

    def returns(year, first, width, blocks, xs):
        part, sums = call(
            functools.partial(returns_body, year, first, secs),
            [shaped(funds, width), shaped(8, funds)],
            [VMEM] * 5,
            "returns",
            scratch=[pltpu.VMEM((total, funds), BF16)] * 4,
            limit=8 * max(1, min(6, total // 512)),
        )(*blocks, xs)
        return part, sums

    firsts = [returns(0, h * half, half, blocks, x_now) for h in range(2)]
    sums = firsts[0][1]
    part = [p for p, _ in firsts]
    peer = [swap(p, 1) for p in part]
    other_sums = swap(sums, 1)

    state = None
    rates = []
    for year in range(years):
        last = year + 1 == years
        if year == 0:
            head = [sums, other_sums]
        else:
            near = [own] + [swap(own, o) for o in SQUARE]
            head = near + [swap(v, 1) for v in near]
        shares = []
        for h in range(1 if last else 2):
            width = paths if last else half
            first = h * half
            pair = [part[h], peer[h]] if year == 0 else [part, peer]
            ins = [me_ref] + head + pair + [draws, member, wides]
            cost = dict(flops=2 * 2 * count * 2 * funds * width, moved=20 * count * width)
            if last:
                ins += [v for s in state for v in s] + [v for rs in rates for v in rs]
                out = [shaped(count, paths), shaped(count, paths), shaped(years, owned, funds)]
                out_specs = [ANY, ANY, VMEM]
                tiles = paths // STEP
                scratch = [pltpu.VMEM((funds, width), F32)]
                scratch += [pltpu.VMEM((tiles, count, STEP), F32)] * 2
                scratch += [pltpu.SemaphoreType.DMA((2, tiles))]
            else:
                ins += ([] if year == 0 else list(state[h])) + [member_t]
                out = [shaped(count, width)] * 2
                out += [shaped(2, 4, 2, slice_funds, width), shaped(owned, funds)]
                out_specs = None
                scratch = [pltpu.VMEM((funds, width), F32), pltpu.VMEM((2, funds, width), F32)]
            shares.append(
                call(
                    functools.partial(year_body, year, first, last, slice_funds),
                    out,
                    [SMEM] + [VMEM] * (len(ins) - 1),
                    "year",
                    scratch=scratch,
                    out_specs=out_specs,
                    limit=16 if last else 8,
                    **cost,
                )(*ins)
            )
        if last:
            assets, liability, credit = shares[0]
            return assets, liability, credit.transpose(0, 2, 1)
        state = [(s[0], s[1]) for s in shares]
        rates.append([s[3] for s in shares])
        held = jnp.concatenate([s[2][0] + swap(s[2][1], 1) for s in shares], -1)
        x_later, held = lax.optimization_barrier((x_later, held))
        if year == 0:
            blocks, held = lax.optimization_barrier((blocks, held))
            others = [swap(b, 1) for b in blocks]
        arrived = [swap(held[i + 1], o) for i, o in enumerate(SQUARE)]
        totals = held[0] + arrived[0] + arrived[1] + arrived[2]
        for o in far[:-1]:
            totals = totals + swap(totals, o)
        totals = [totals] + [swap(totals, o) for o in far[-1:]]
        part = returns(year + 1, 0, paths, blocks, x_later)[0]
        peer = returns(year + 1, 0, paths, others, x_later)[0]
        own = call(
            functools.partial(own_body, slice_funds),
            shaped(slice_funds, paths),
            [SMEM] + [VMEM] * (2 + len(totals)),
            "own",
            10**6,
            10**6,
            limit=2,
        )(me_ref, part, peer, *totals)


def solution(mesh):
    in_specs = (
        P("grp", None, None),
        P("pol", None),
        P("pol"),
        P("pol", None),
        P("pol", None),
        P("pol"),
        P("pol"),
        P("pol"),
        P("pol"),
        P(),
        P(),
        P("pol", "grp", None),
    )
    out_specs = (P("pol", "grp"), P("pol", "grp"), P("grp", None, "pol"))
    return jax.shard_map(local, mesh=mesh, in_specs=in_specs, out_specs=out_specs, check_vma=False)
```

```python
import functools

import jax
import jax.numpy as jnp
from jax import lax
from jax.experimental import pallas as pl
from jax.experimental.pallas import tpu as pltpu
from jax.sharding import PartitionSpec as P

F32, BF16 = jnp.float32, jnp.bfloat16
SQUARE = (2, 4, 6)
VMEM = pl.BlockSpec(memory_space=pltpu.VMEM)
SMEM = pl.BlockSpec(memory_space=pltpu.SMEM)
ANY = pl.BlockSpec(memory_space=pl.ANY)
HBM = pl.BlockSpec(memory_space=pltpu.HBM)
ROW = (((1,), (1,)), ((), ()))


def swap(x, offset):
    n = lax.axis_size("pol")
    return lax.ppermute(x, "pol", [(i, i ^ offset) for i in range(n)])


def far_offsets():
    n = lax.axis_size("pol")
    return [1 << b for b in range(3, n.bit_length() - 1)]


def rate(ratio):
    x = 20.0 * (ratio - 1.05)
    return 0.01 + (jnp.maximum(x, 0.0) + jnp.log1p(jnp.exp(-jnp.abs(x)))) / 20.0


def halves(v):
    hi = v.astype(BF16)
    return hi, (v - hi.astype(F32)).astype(BF16)


def dot(a, b, dims=(((1,), (0,)), ((), ()))):
    return lax.dot_general(a, b, dims, preferred_element_type=F32)


def call(body, out, ins, name, flops=0, moved=0, scratch=(), out_specs=None, limit=24):
    return pl.pallas_call(
        body,
        out_shape=out,
        in_specs=ins,
        out_specs=out_specs if out_specs is not None else jax.tree.map(lambda _: VMEM, out),
        scratch_shapes=scratch,
        compiler_params=pltpu.CompilerParams(vmem_limit_bytes=int(limit * 2**20)),
        cost_estimate=pl.CostEstimate(flops=flops, bytes_accessed=moved, transcendentals=0),
        name=name,
    )


def shaped(*dims, dtype=F32):
    return jax.ShapeDtypeStruct(dims, dtype)


def pack_body(*refs):
    sources, (out, lines), held, sem = refs[1:11], refs[11:13], refs[13:23], refs[23]
    copies = [pltpu.make_async_copy(s, h, sem.at[i]) for i, (s, h) in enumerate(zip(sources, held))]
    for copy in copies:
        copy.start()
    for copy in copies:
        copy.wait()
    load, hold, drift, fund, term, asset, liab, kind, base, guar = held
    secs, funds = load.shape
    count = fund.shape[1]
    out[0:secs, :] = load[...]
    out[secs : 2 * secs, :] = hold[...]
    member = (lax.broadcasted_iota(jnp.int32, (funds, count), 0) == fund[...]).astype(BF16)
    at = lax.broadcasted_iota(jnp.int32, (8, count), 0)
    alive = (term[...] > 0).astype(F32)
    v = jnp.where(at < 3, asset[...] * alive, liab[...])
    one, rest = v.astype(BF16).astype(F32), v - v.astype(BF16).astype(F32)
    two = rest.astype(BF16).astype(F32)
    three = rest - two
    spot = jnp.where(at < 3, at, at - 3)
    rows = jnp.where(spot == 0, one, jnp.where(spot == 1, two, three))
    rows = jnp.where(at < 6, rows, 0.0).astype(BF16)
    out[2 * secs : 2 * secs + 8, :] = dot(rows, member, ROW)
    fixed = jnp.dot(
        jnp.broadcast_to(drift[...], (8, secs)), hold[...], precision=lax.Precision.HIGHEST
    )
    out[2 * secs + 6 : 2 * secs + 7, :] = fixed[0:1, :]
    base_row = jnp.zeros((1, count), F32)
    guar_row = jnp.zeros((1, count), F32)
    for t in range(base.shape[1]):
        base_row = jnp.where(kind[...] == t, base[:, t : t + 1], base_row)
        guar_row = jnp.where(kind[...] == t, guar[:, t : t + 1], guar_row)
    values = (fund[...].astype(F32), term[...].astype(F32), base_row, guar_row, asset[...], liab[...])
    stack = jnp.zeros((8, count), F32)
    for r, row in enumerate(values):
        stack = jnp.where(at == r, row, stack)
    lines[...] = stack


def columns_body(lines, block, shocks, member_t, member, wides, x_now, x_later, own, raw, sem):
    own[0] = block[...]
    years, funds, count = member_t.shape
    fetch = pltpu.make_async_copy(shocks, raw, sem)
    fetch.start()
    stack = jnp.concatenate([lines[...], jnp.zeros((120, count), F32)], 0)
    cols = jnp.transpose(stack)
    wide = lambda r: jnp.broadcast_to(cols[:, r : r + 1], (count, 128))
    fund_c, term_c, base_c, guar_c = wide(0), wide(1), wide(2), wide(3)
    wides[2 * years] = wide(4)
    wides[2 * years + 1] = wide(5)
    hot_t = lax.broadcasted_iota(jnp.int32, (funds, count), 0).astype(F32) == lines[0:1, :]
    hot = lax.broadcasted_iota(jnp.int32, (count, funds), 1).astype(F32) == fund_c
    for y in range(years):
        alive = term_c > float(y)
        wides[2 * y] = jnp.where(alive, base_c, 0.0)
        wides[2 * y + 1] = jnp.where(alive, guar_c, 0.0)
        here = jnp.logical_and(hot, alive).astype(F32).astype(BF16)
        member[y, :, 0:funds] = here
        member[y, :, funds : 2 * funds] = here
        if y == 0:
            member_t[y] = hot_t.astype(F32).astype(BF16)
        else:
            member_t[y] = jnp.logical_and(hot_t, lines[1:2, :] > float(y)).astype(F32).astype(BF16)
    fetch.wait()
    for y in range(years):
        hi, lo = halves(raw[y])
        if y == 0:
            x_now[0], x_now[1] = hi, lo
        else:
            x_later[y - 1, 0], x_later[y - 1, 1] = hi, lo


def returns_body(year, first, secs, begun, final, *refs):
    *blocks, xs, part, sums, load_hi, load_lo, held, flip_hi, flip_lo = refs
    if begun:
        *blocks, before, sums_before = blocks
    funds, width = part.shape
    total = load_hi.shape[0]
    at = 0
    extra = sums_before[...] if begun else jnp.zeros((8, funds), F32)
    for block in blocks:
        for b in range(block.shape[0]):
            load_hi[at : at + secs, :], load_lo[at : at + secs, :] = halves(block[b, 0:secs, :])
            held[at : at + secs, :] = block[b, secs : 2 * secs, :]
            extra = extra + block[b, 2 * secs : 2 * secs + 8, :]
            at += secs
    sums[...] = extra
    for g in range(0, total, 128):
        flip_hi[:, g : g + 128], flip_lo[:, g : g + 128] = halves(jnp.transpose(held[g : g + 128, :]))
    if final:
        row = lax.broadcasted_iota(jnp.int32, (128, funds), 0)
        fixed = jnp.transpose(jnp.where(row == 0, extra[6:7, :], 0.0))[:, 0:1]
    step = min(256, width)
    group = min(512, total)

    def exposed(c, g):
        cut = slice(first + c, first + c + step)
        x_hi, x_lo = (xs[i, :, cut] if year == 0 else xs[year - 1, i, :, cut] for i in range(2))
        lh, ll = load_hi[g : g + group, :], load_lo[g : g + group, :]
        return dot(jnp.concatenate([lh, lh], 1), jnp.concatenate([x_hi, x_lo], 0)) + dot(ll, x_hi)

    spots = [(c, g) for c in range(0, width, step) for g in range(0, total, group)]
    ahead = exposed(*spots[0])
    for i, (c, g) in enumerate(spots):
        now = ahead
        ahead = exposed(*spots[i + 1]) if i + 1 < len(spots) else None
        t_hi, t_lo = halves(jnp.tanh(now))
        fh, fl = flip_hi[:, g : g + group], flip_lo[:, g : g + group]
        new = 0.25 * dot(jnp.concatenate([fh, fh, fl], 1), jnp.concatenate([t_hi, t_lo, t_hi], 0))
        acc = new if g == 0 else acc + new
        if g + group == total:
            if begun:
                acc = acc + before[:, first + c : first + c + step]
            part[:, c : c + step] = acc + fixed if final else acc


def own_columns(me_ref, declared, first, out):
    paths, funds = out.shape
    width = declared.shape[1]
    spot = lax.broadcasted_iota(jnp.int32, (paths, width), 1) + first
    pick = spot == lax.broadcasted_iota(jnp.int32, (paths, width), 0) + me_ref[0] * paths
    pick = pick.astype(F32).astype(BF16)
    one, rest = declared.astype(BF16), declared - declared.astype(BF16).astype(F32)
    two, three = halves(rest)
    out[...] = dot(pick, one, ROW) + dot(pick, two, ROW) + dot(pick, three, ROW)


def slice_spot(me_ref, order, slice_funds):
    label = (order >> 2) | ((order & 3) << 1)
    return pl.multiple_of(((me_ref[0] & 7) ^ label) * slice_funds, slice_funds)


def advance(step, got, base, guar, draw, asset, liab):
    wide = lambda v: jnp.concatenate([v] * (step // 128), 1)
    growth, credit = got[:, 0:step], jnp.maximum(got[:, step:], wide(guar))
    lapse = jnp.minimum(wide(base) * (0.5 + draw.astype(F32)) * jnp.exp(5.0 * (growth - credit)), 0.5)
    stay = 1.0 - lapse
    return asset * (1.0 + growth) * stay, liab * (1.0 + credit) * stay


def table_of(growth, declared):
    g_hi, g_lo = halves(growth)
    d_hi, d_lo = halves(declared)
    return jnp.concatenate([jnp.concatenate([g_hi, d_hi], 1), jnp.concatenate([g_lo, d_lo], 1)], 0)


def own_body(slice_funds, me, part, peer, *refs):
    totals, out = refs[:-1], refs[-1]
    rows = pl.ds(pl.multiple_of((me[0] & 7) * slice_funds, slice_funds), slice_funds)
    growth = part[rows, :] + peer[rows, :]
    asset, liab = totals[0][0], totals[0][1]
    for t in totals[1:]:
        asset, liab = asset + t[0], liab + t[1]
    out[...] = rate(asset * (1.0 + growth) / liab)


STEP, ROWS = 256, 512


def year_body(year, first, last, slice_funds, *refs):
    refs = list(refs)
    me = refs.pop(0)
    if year == 0:
        mine, other = refs.pop(0), refs.pop(0)
    else:
        slices = [refs.pop(0) for _ in range(8)]
    part, peer = refs.pop(0), refs.pop(0)
    draws, member, wides = refs.pop(0), refs.pop(0), refs.pop(0)
    states = [(refs.pop(0), refs.pop(0)) for _ in range(0 if year == 0 else 2 if last else 1)]
    lead = 0
    if last:
        earlier = [refs.pop(0) for _ in range(2 * year)]
        out_a, out_l, out_r, declared, buf_a, buf_l, sem = refs
    else:
        member_t = refs.pop(0)
        out_a, out_l, out_s, out_r, declared, acc = refs
    funds, width = declared.shape
    count = member.shape[1]
    if year == 0:
        sums = mine[...] + other[...]
        row = lax.broadcasted_iota(jnp.int32, (128, funds), 0)
        start_a = sums[0:1, :] + sums[1:2, :] + sums[2:3, :]
        start_l = sums[3:4, :] + sums[4:5, :] + sums[5:6, :]
        both = jnp.where(row == 0, start_a, jnp.where(row == 1, start_l, 0.0))
        both = jnp.transpose(both)
        ratio = both[:, 0:1] / both[:, 1:2]
        declared[...] = rate(ratio * (1.0 + (part[...] + peer[...])))
    else:
        lead = first
        for o in range(8):
            spot = pl.ds(slice_spot(me, o, slice_funds), slice_funds)
            declared[spot, :] = slices[o][:, first : first + width]
    if last:
        own = out_r.at[year]
        for y in range(year):
            out_r[y] = earlier[2 * y][...] + earlier[2 * y + 1][...]
    else:
        own = out_r
    copies = []

    def gathered(c):
        there = slice(lead + c, lead + c + STEP)
        table = table_of(part[:, there] + peer[:, there], declared[:, c : c + STEP])
        return [dot(member[year, r : r + ROWS, :], table) for r in range(0, count, ROWS)]

    ahead = gathered(0)
    for c in range(0, width, STEP):
        cut = slice(c, c + STEP)
        now = ahead
        ahead = gathered(c + STEP) if c + STEP < width else None
        sum_a = sum_l = None
        for r in range(0, count, ROWS):
            rows = slice(r, r + ROWS)
            if year == 0:
                years = member.shape[0]
                asset = jnp.concatenate([wides[2 * years, rows, :]] * (STEP // 128), 1)
                liab = jnp.concatenate([wides[2 * years + 1, rows, :]] * (STEP // 128), 1)
            else:
                half = states[0][0].shape[1]
                held = states[c // half]
                at = slice(c % half, c % half + STEP)
                asset, liab = held[0][rows, at], held[1][rows, at]
            asset, liab = advance(
                STEP, now[r // ROWS], wides[2 * year, rows, :], wides[2 * year + 1, rows, :],
                draws[year, rows, first + c : first + c + STEP], asset, liab,
            )
            if last:
                buf_a[c // STEP, rows, :] = asset
                buf_l[c // STEP, rows, :] = liab
            else:
                out_a[rows, cut] = asset
                out_l[rows, cut] = liab
                a_hi, a_lo = halves(asset)
                l_hi, l_lo = halves(liab)
                ma, ml = member_t[year + 1, :, rows], member_t[0, :, rows]
                add_a = dot(jnp.concatenate([ma, ma], 1), jnp.concatenate([a_hi, a_lo], 0))
                add_l = dot(jnp.concatenate([ml, ml], 1), jnp.concatenate([l_hi, l_lo], 0))
                sum_a = add_a if sum_a is None else sum_a + add_a
                sum_l = add_l if sum_l is None else sum_l + add_l
        if last:
            for buf, out, k in ((buf_a, out_a, 0), (buf_l, out_l, 1)):
                copy = pltpu.make_async_copy(buf.at[c // STEP], out.at[:, cut], sem.at[k, c // STEP])
                copy.start()
                copies.append(copy)
        else:
            acc[0, :, cut] = sum_a
            acc[1, :, cut] = sum_l
    own_columns(me, declared[...], first, own)
    if last:
        for copy in copies:
            copy.wait()
    else:
        for o in range(8):
            for v in range(2):
                out_s[o // 4, o % 4, v] = acc[v, pl.ds(slice_spot(me, o, slice_funds), slice_funds), :]


def local(
    shocks,
    loadings,
    sec_drift,
    holdings,
    fund_of,
    product_type,
    term_years,
    asset_start,
    liab_start,
    base_lapse,
    guarantee,
    lapse_draw,
):
    years, _, paths = shocks.shape
    secs, funds = holdings.shape
    count = asset_start.shape[0]
    n = lax.axis_size("pol")
    me = lax.axis_index("pol")
    me_ref = me.astype(jnp.int32).reshape(1)
    slice_funds = funds // 8
    owned = paths // n
    half = paths // 2
    draws = lapse_draw.transpose(1, 0, 2)
    line = lambda v: v.reshape(1, count)
    fund, kind, term = line(fund_of), line(product_type), line(term_years)
    asset, liab = line(asset_start), line(liab_start)

    sources = [loadings, holdings, sec_drift.reshape(1, secs), fund, term, asset, liab, kind]
    sources += [base_lapse.reshape(1, -1), guarantee.reshape(1, -1)]
    block, lines = call(
        pack_body,
        [shaped(2 * secs + 8, funds), shaped(8, count)],
        [SMEM] + [HBM] * 10,
        "pack",
        10**6,
        10**5,
        scratch=[pltpu.VMEM(v.shape, v.dtype) for v in sources] + [pltpu.SemaphoreType.DMA((10,))],
        limit=60,
    )(me_ref, *sources)
    far = far_offsets()
    came = swap(block[None], far[-1])
    member_t, member, wides, x_now, x_later, block = call(
        columns_body,
        [
            shaped(years, funds, count, dtype=BF16),
            shaped(years, count, 2 * funds, dtype=BF16),
            shaped(2 * years + 2, count, 128),
            shaped(2, *shocks.shape[1:], dtype=BF16),
            shaped(years - 1, 2, *shocks.shape[1:], dtype=BF16),
            shaped(1, *block.shape),
        ],
        [VMEM, VMEM, HBM],
        "columns",
        10**6,
        4 * 10**6,
        scratch=[pltpu.VMEM(shocks.shape, F32), pltpu.SemaphoreType.DMA],
        limit=8,
    )(lines, block, shocks)
    came, block = lax.optimization_barrier((came, block))
    block = jnp.concatenate([block, came])
    for o in reversed(far[:-1]):
        block = jnp.concatenate([block, swap(block, o)])
    blocks = [block] + [swap(block, o) for o in SQUARE]

    def returns(year, first, width, blocks, xs, before=(), final=True):
        total = secs * sum(b.shape[0] for b in blocks)
        return call(
            functools.partial(returns_body, year, first, secs, len(before) > 0, final),
            [shaped(funds, width), shaped(8, funds)],
            [VMEM] * (len(blocks) + len(before) + 1),
            "returns",
            scratch=[pltpu.VMEM((total, funds), BF16)] * 2
            + [pltpu.VMEM((total, funds), F32)]
            + [pltpu.VMEM((funds, total), BF16)] * 2,
            limit=8 * max(1, min(6, total // 512)),
        )(*blocks, *before, xs)

    before = ()
    for b in blocks[:-1]:
        before = returns(0, 0, paths, [b], x_now, before, False)
    firsts = [returns(0, h * half, half, blocks[-1:], x_now, before) for h in range(2)]
    sums = firsts[0][1]
    part = [p for p, _ in firsts]
    peer = [swap(p, 1) for p in part]
    other_sums = swap(sums, 1)

    state = None
    rates = []
    for year in range(years):
        last = year + 1 == years
        if year == 0:
            head = [sums, other_sums]
        else:
            near = [own] + [swap(own, o) for o in SQUARE]
            head = near + [swap(v, 1) for v in near]
        shares = []
        for h in range(1 if last else 2):
            width = paths if last else half
            first = h * half
            pair = [part[h], peer[h]] if year == 0 else [part, peer]
            ins = [me_ref] + head + pair + [draws, member, wides]
            cost = dict(flops=2 * 2 * count * 2 * funds * width, moved=20 * count * width)
            if last:
                ins += [v for s in state for v in s] + [v for rs in rates for v in rs]
                out = [shaped(count, paths), shaped(count, paths), shaped(years, owned, funds)]
                out_specs = [ANY, ANY, VMEM]
                tiles = paths // STEP
                scratch = [pltpu.VMEM((funds, width), F32)]
                scratch += [pltpu.VMEM((tiles, count, STEP), F32)] * 2
                scratch += [pltpu.SemaphoreType.DMA((2, tiles))]
            else:
                ins += ([] if year == 0 else list(state[h])) + [member_t]
                out = [shaped(count, width)] * 2
                out += [shaped(2, 4, 2, slice_funds, width), shaped(owned, funds)]
                out_specs = None
                scratch = [pltpu.VMEM((funds, width), F32), pltpu.VMEM((2, funds, width), F32)]
            shares.append(
                call(
                    functools.partial(year_body, year, first, last, slice_funds),
                    out,
                    [SMEM] + [VMEM] * (len(ins) - 1),
                    "year",
                    scratch=scratch,
                    out_specs=out_specs,
                    limit=16 if last else 8,
                    **cost,
                )(*ins)
            )
        if last:
            assets, liability, credit = shares[0]
            return assets, liability, credit.transpose(0, 2, 1)
        state = [(s[0], s[1]) for s in shares]
        rates.append([s[3] for s in shares])
        held = jnp.concatenate([s[2][0] + swap(s[2][1], 1) for s in shares], -1)
        x_later, held = lax.optimization_barrier((x_later, held))
        if year == 0:
            blocks, held = lax.optimization_barrier((blocks, held))
            others = [swap(b, 1) for b in blocks]
        arrived = [swap(held[i + 1], o) for i, o in enumerate(SQUARE)]
        totals = held[0] + arrived[0] + arrived[1] + arrived[2]
        for o in far[:-1]:
            totals = totals + swap(totals, o)
        totals = [totals] + [swap(totals, o) for o in far[-1:]]
        part = returns(year + 1, 0, paths, blocks, x_later)[0]
        peer = returns(year + 1, 0, paths, others, x_later)[0]
        own = call(
            functools.partial(own_body, slice_funds),
            shaped(slice_funds, paths),
            [SMEM] + [VMEM] * (2 + len(totals)),
            "own",
            10**6,
            10**6,
            limit=2,
        )(me_ref, part, peer, *totals)


def solution(mesh):
    in_specs = (
        P("grp", None, None),
        P("pol", None),
        P("pol"),
        P("pol", None),
        P("pol", None),
        P("pol"),
        P("pol"),
        P("pol"),
        P("pol"),
        P(),
        P(),
        P("pol", "grp", None),
    )
    out_specs = (P("pol", "grp"), P("pol", "grp"), P("grp", None, "pol"))
    return jax.shard_map(local, mesh=mesh, in_specs=in_specs, out_specs=out_specs, check_vma=False)
```

```python
import functools

import jax
import jax.numpy as jnp
from jax import lax
from jax.experimental import pallas as pl
from jax.experimental.pallas import tpu as pltpu
from jax.sharding import PartitionSpec as P

F32, BF16 = jnp.float32, jnp.bfloat16
SQUARE = (2, 4, 6)
FIRST = (2, 4)
FULL = ((4, 8), (8, 2))
VMEM = pl.BlockSpec(memory_space=pltpu.VMEM)
SMEM = pl.BlockSpec(memory_space=pltpu.SMEM)
ANY = pl.BlockSpec(memory_space=pl.ANY)
HBM = pl.BlockSpec(memory_space=pltpu.HBM)
ROW = (((1,), (1,)), ((), ()))


def swap(x, offset, odd=None):
    n = lax.axis_size("pol")
    offsets = (offset, offset if odd is None else odd)
    return lax.ppermute(x, "pol", [(i, i ^ offsets[i % 2]) for i in range(n)])


def tie(x, other):
    return lax.optimization_barrier((x, other))[0]


def far_offsets():
    n = lax.axis_size("pol")
    return [1 << b for b in range(3, n.bit_length() - 1)]


def rate(ratio):
    x = 20.0 * (ratio - 1.05)
    return 0.01 + (jnp.maximum(x, 0.0) + jnp.log1p(jnp.exp(-jnp.abs(x)))) / 20.0


def halves(v):
    hi = v.astype(BF16)
    return hi, (v - hi.astype(F32)).astype(BF16)


def dot(a, b, dims=(((1,), (0,)), ((), ()))):
    return lax.dot_general(a, b, dims, preferred_element_type=F32)


def call(body, out, ins, name, flops=0, moved=0, scratch=(), out_specs=None, limit=24):
    return pl.pallas_call(
        body,
        out_shape=out,
        in_specs=ins,
        out_specs=out_specs if out_specs is not None else jax.tree.map(lambda _: VMEM, out),
        scratch_shapes=scratch,
        compiler_params=pltpu.CompilerParams(vmem_limit_bytes=int(limit * 2**20)),
        cost_estimate=pl.CostEstimate(flops=flops, bytes_accessed=moved, transcendentals=0),
        name=name,
    )


def shaped(*dims, dtype=F32):
    return jax.ShapeDtypeStruct(dims, dtype)


def pack_body(*refs):
    sources, (out, lines), held, sem = refs[1:11], refs[11:13], refs[13:23], refs[23]
    copies = [pltpu.make_async_copy(s, h, sem.at[i]) for i, (s, h) in enumerate(zip(sources, held))]
    for copy in copies:
        copy.start()
    for copy in copies:
        copy.wait()
    load, hold, drift, fund, term, asset, liab, kind, base, guar = held
    secs, funds = load.shape
    count = fund.shape[1]
    out[0:secs, :] = load[...]
    out[secs : 2 * secs, :] = hold[...]
    member = (lax.broadcasted_iota(jnp.int32, (funds, count), 0) == fund[...]).astype(BF16)
    at = lax.broadcasted_iota(jnp.int32, (8, count), 0)
    alive = (term[...] > 0).astype(F32)
    v = jnp.where(at < 3, asset[...] * alive, liab[...])
    one, rest = v.astype(BF16).astype(F32), v - v.astype(BF16).astype(F32)
    two = rest.astype(BF16).astype(F32)
    three = rest - two
    spot = jnp.where(at < 3, at, at - 3)
    rows = jnp.where(spot == 0, one, jnp.where(spot == 1, two, three))
    rows = jnp.where(at < 6, rows, 0.0).astype(BF16)
    out[2 * secs : 2 * secs + 8, :] = dot(rows, member, ROW)
    fixed = jnp.dot(
        jnp.broadcast_to(drift[...], (8, secs)), hold[...], precision=lax.Precision.HIGHEST
    )
    out[2 * secs + 6 : 2 * secs + 7, :] = fixed[0:1, :]
    base_row = jnp.zeros((1, count), F32)
    guar_row = jnp.zeros((1, count), F32)
    for t in range(base.shape[1]):
        base_row = jnp.where(kind[...] == t, base[:, t : t + 1], base_row)
        guar_row = jnp.where(kind[...] == t, guar[:, t : t + 1], guar_row)
    values = (fund[...].astype(F32), term[...].astype(F32), base_row, guar_row, asset[...], liab[...])
    stack = jnp.zeros((8, count), F32)
    for r, row in enumerate(values):
        stack = jnp.where(at == r, row, stack)
    lines[...] = stack


def columns_body(lines, block, shocks, member_t, member, wides, x_now, x_later, own, raw, sem):
    own[0] = block[...]
    years, funds, count = member_t.shape
    fetch = pltpu.make_async_copy(shocks, raw, sem)
    fetch.start()
    stack = jnp.concatenate([lines[...], jnp.zeros((120, count), F32)], 0)
    cols = jnp.transpose(stack)
    wide = lambda r: jnp.broadcast_to(cols[:, r : r + 1], (count, 128))
    fund_c, term_c, base_c, guar_c = wide(0), wide(1), wide(2), wide(3)
    wides[2 * years] = wide(4)
    wides[2 * years + 1] = wide(5)
    hot_t = lax.broadcasted_iota(jnp.int32, (funds, count), 0).astype(F32) == lines[0:1, :]
    hot = lax.broadcasted_iota(jnp.int32, (count, funds), 1).astype(F32) == fund_c
    for y in range(years):
        alive = term_c > float(y)
        wides[2 * y] = jnp.where(alive, base_c, 0.0)
        wides[2 * y + 1] = jnp.where(alive, guar_c, 0.0)
        here = jnp.logical_and(hot, alive).astype(F32).astype(BF16)
        member[y, :, 0:funds] = here
        member[y, :, funds : 2 * funds] = here
        if y == 0:
            member_t[y] = hot_t.astype(F32).astype(BF16)
        else:
            member_t[y] = jnp.logical_and(hot_t, lines[1:2, :] > float(y)).astype(F32).astype(BF16)
    fetch.wait()
    for y in range(years):
        hi, lo = halves(raw[y])
        if y == 0:
            x_now[0], x_now[1] = hi, lo
        else:
            x_later[y - 1, 0], x_later[y - 1, 1] = hi, lo


def returns_body(year, first, secs, begun, final, *refs):
    *blocks, xs, part, sums, load_hi, load_lo, held, flip_hi, flip_lo = refs
    if begun:
        *blocks, before, sums_before = blocks
    funds, width = part.shape
    total = load_hi.shape[0]
    at = 0
    extra = sums_before[...] if begun else jnp.zeros((8, funds), F32)
    for block in blocks:
        for b in range(block.shape[0]):
            load_hi[at : at + secs, :], load_lo[at : at + secs, :] = halves(block[b, 0:secs, :])
            held[at : at + secs, :] = block[b, secs : 2 * secs, :]
            extra = extra + block[b, 2 * secs : 2 * secs + 8, :]
            at += secs
    sums[...] = extra
    for g in range(0, total, 128):
        flip_hi[:, g : g + 128], flip_lo[:, g : g + 128] = halves(jnp.transpose(held[g : g + 128, :]))
    if final:
        row = lax.broadcasted_iota(jnp.int32, (128, funds), 0)
        fixed = jnp.transpose(jnp.where(row == 0, extra[6:7, :], 0.0))[:, 0:1]
    step = min(256, width)
    group = min(512, total)

    def exposed(c, g):
        cut = slice(first + c, first + c + step)
        x_hi, x_lo = (xs[i, :, cut] if year == 0 else xs[year - 1, i, :, cut] for i in range(2))
        lh, ll = load_hi[g : g + group, :], load_lo[g : g + group, :]
        return dot(jnp.concatenate([lh, lh], 1), jnp.concatenate([x_hi, x_lo], 0)) + dot(ll, x_hi)

    spots = [(c, g) for c in range(0, width, step) for g in range(0, total, group)]
    ahead = exposed(*spots[0])
    for i, (c, g) in enumerate(spots):
        now = ahead
        ahead = exposed(*spots[i + 1]) if i + 1 < len(spots) else None
        t_hi, t_lo = halves(jnp.tanh(now))
        fh, fl = flip_hi[:, g : g + group], flip_lo[:, g : g + group]
        new = 0.25 * dot(jnp.concatenate([fh, fh, fl], 1), jnp.concatenate([t_hi, t_lo, t_hi], 0))
        acc = new if g == 0 else acc + new
        if g + group == total:
            if begun:
                acc = acc + before[:, first + c : first + c + step]
            part[:, c : c + step] = acc + fixed if final else acc


def own_columns(me_ref, declared, first, out):
    paths, funds = out.shape
    width = declared.shape[1]
    spot = lax.broadcasted_iota(jnp.int32, (paths, width), 1) + first
    pick = spot == lax.broadcasted_iota(jnp.int32, (paths, width), 0) + me_ref[0] * paths
    pick = pick.astype(F32).astype(BF16)
    one, rest = declared.astype(BF16), declared - declared.astype(BF16).astype(F32)
    two, three = halves(rest)
    out[...] = dot(pick, one, ROW) + dot(pick, two, ROW) + dot(pick, three, ROW)


def slice_spot(me, order, slice_funds):
    core = (me & 1) ^ (order >> 1)
    side = ((me >> (1 + core)) & 1) ^ (order & 1)
    return pl.multiple_of((2 * core + side) * slice_funds, slice_funds)


def advance(step, got, base, guar, draw, asset, liab):
    wide = lambda v: jnp.concatenate([v] * (step // 128), 1)
    growth, credit = got[:, 0:step], jnp.maximum(got[:, step:], wide(guar))
    lapse = jnp.minimum(wide(base) * (0.5 + draw.astype(F32)) * jnp.exp(5.0 * (growth - credit)), 0.5)
    stay = 1.0 - lapse
    return asset * (1.0 + growth) * stay, liab * (1.0 + credit) * stay


def table_of(growth, declared):
    g_hi, g_lo = halves(growth)
    d_hi, d_lo = halves(declared)
    return jnp.concatenate([jnp.concatenate([g_hi, d_hi], 1), jnp.concatenate([g_lo, d_lo], 1)], 0)


def own_body(slice_funds, first, me, part, peer, *refs):
    totals, out = refs[:-1], refs[-1]
    rows = pl.ds(slice_spot(me[0], 0, slice_funds), slice_funds)
    cut = slice(first, first + out.shape[1])
    growth = part[rows, cut] + peer[rows, cut]
    asset, liab = totals[0][0], totals[0][1]
    for t in totals[1:]:
        asset, liab = asset + t[0], liab + t[1]
    out[...] = rate(asset * (1.0 + growth) / liab)


STEP, ROWS = 256, 512


def year_body(year, first, last, slice_funds, *refs):
    refs = list(refs)
    me = refs.pop(0)
    if year == 0:
        mine, other = refs.pop(0), refs.pop(0)
    else:
        slices = [refs.pop(0) for _ in range(4)]
    part, peer = refs.pop(0), refs.pop(0)
    draws, member, wides = refs.pop(0), refs.pop(0), refs.pop(0)
    held = [refs.pop(0) for _ in range(2 if year else 0)]
    lead = 0
    copies = []
    if last and first:
        half_a, half_l, *earlier, out_a, out_l, out_r, declared, buf_a, buf_l, sem = refs
        own = out_r.at[year]
        for k, (half, out) in enumerate(((half_a, out_a), (half_l, out_l))):
            copies.append(pltpu.make_async_copy(half, out.at[:, 0:first], sem.at[k, 0]))
            copies[-1].start()
    elif last:
        out_a, out_l, own, declared = refs
    else:
        member_t = refs.pop(0)
        out_a, out_l, out_s, own, declared, acc = refs
    funds, width = declared.shape
    count = member.shape[1]
    if year == 0:
        sums = mine[...] + other[...]
        row = lax.broadcasted_iota(jnp.int32, (128, funds), 0)
        start_a = sums[0:1, :] + sums[1:2, :] + sums[2:3, :]
        start_l = sums[3:4, :] + sums[4:5, :] + sums[5:6, :]
        both = jnp.where(row == 0, start_a, jnp.where(row == 1, start_l, 0.0))
        both = jnp.transpose(both)
        ratio = both[:, 0:1] / both[:, 1:2]
        declared[...] = rate(ratio * (1.0 + (part[...] + peer[...])))
    else:
        lead = first
        for o in range(4):
            declared[pl.ds(slice_spot(me[0], o, slice_funds), slice_funds), :] = slices[o][...]
    if last and first:
        for y in range(year):
            out_r[y] = earlier[2 * y][...] + earlier[2 * y + 1][...]

    def gathered(c):
        there = slice(lead + c, lead + c + STEP)
        table = table_of(part[:, there] + peer[:, there], declared[:, c : c + STEP])
        return [dot(member[year, r : r + ROWS, :], table) for r in range(0, count, ROWS)]

    ahead = gathered(0)
    for c in range(0, width, STEP):
        cut = slice(c, c + STEP)
        now = ahead
        ahead = gathered(c + STEP) if c + STEP < width else None
        sum_a = sum_l = None
        for r in range(0, count, ROWS):
            rows = slice(r, r + ROWS)
            if year == 0:
                years = member.shape[0]
                asset = jnp.concatenate([wides[2 * years, rows, :]] * (STEP // 128), 1)
                liab = jnp.concatenate([wides[2 * years + 1, rows, :]] * (STEP // 128), 1)
            else:
                asset, liab = held[0][rows, cut], held[1][rows, cut]
            asset, liab = advance(
                STEP, now[r // ROWS], wides[2 * year, rows, :], wides[2 * year + 1, rows, :],
                draws[year, rows, first + c : first + c + STEP], asset, liab,
            )
            if last and first:
                buf_a[c // STEP, rows, :] = asset
                buf_l[c // STEP, rows, :] = liab
            else:
                out_a[rows, cut] = asset
                out_l[rows, cut] = liab
            if not last:
                a_hi, a_lo = halves(asset)
                l_hi, l_lo = halves(liab)
                ma, ml = member_t[year + 1, :, rows], member_t[0, :, rows]
                add_a = dot(jnp.concatenate([ma, ma], 1), jnp.concatenate([a_hi, a_lo], 0))
                add_l = dot(jnp.concatenate([ml, ml], 1), jnp.concatenate([l_hi, l_lo], 0))
                sum_a = add_a if sum_a is None else sum_a + add_a
                sum_l = add_l if sum_l is None else sum_l + add_l
        if last and first:
            for buf, out, k in ((buf_a, out_a, 0), (buf_l, out_l, 1)):
                copy = pltpu.make_async_copy(
                    buf.at[c // STEP], out.at[:, first + c : first + c + STEP], sem.at[k, 1 + c // STEP]
                )
                copy.start()
                copies.append(copy)
        elif not last:
            acc[0, :, cut] = sum_a
            acc[1, :, cut] = sum_l
    own_columns(me, declared[...], first, own)
    if last and first:
        out_r[year] = out_r[year] + earlier[2 * year][...]
    for copy in copies:
        copy.wait()
    if not last:
        for o in range(4):
            for v in range(2):
                spot = pl.ds(slice_spot(me[0], o, slice_funds), slice_funds)
                out_s[o // 2, o % 2, v] = acc[v, spot, :]


def local(
    shocks,
    loadings,
    sec_drift,
    holdings,
    fund_of,
    product_type,
    term_years,
    asset_start,
    liab_start,
    base_lapse,
    guarantee,
    lapse_draw,
):
    years, _, paths = shocks.shape
    secs, funds = holdings.shape
    count = asset_start.shape[0]
    n = lax.axis_size("pol")
    me = lax.axis_index("pol")
    me_ref = me.astype(jnp.int32).reshape(1)
    slice_funds = funds // 4
    owned = paths // n
    half = paths // 2
    draws = lapse_draw.transpose(1, 0, 2)
    line = lambda v: v.reshape(1, count)
    fund, kind, term = line(fund_of), line(product_type), line(term_years)
    asset, liab = line(asset_start), line(liab_start)

    sources = [loadings, holdings, sec_drift.reshape(1, secs), fund, term, asset, liab, kind]
    sources += [base_lapse.reshape(1, -1), guarantee.reshape(1, -1)]
    block, lines = call(
        pack_body,
        [shaped(2 * secs + 8, funds), shaped(8, count)],
        [SMEM] + [HBM] * 10,
        "pack",
        10**6,
        10**5,
        scratch=[pltpu.VMEM(v.shape, v.dtype) for v in sources] + [pltpu.SemaphoreType.DMA((10,))],
        limit=60,
    )(me_ref, *sources)
    far = far_offsets()
    came = swap(block[None], far[-1])
    member_t, member, wides, x_now, x_later, block = call(
        columns_body,
        [
            shaped(years, funds, count, dtype=BF16),
            shaped(years, count, 2 * funds, dtype=BF16),
            shaped(2 * years + 2, count, 128),
            shaped(2, *shocks.shape[1:], dtype=BF16),
            shaped(years - 1, 2, *shocks.shape[1:], dtype=BF16),
            shaped(1, *block.shape),
        ],
        [VMEM, VMEM, HBM],
        "columns",
        10**6,
        4 * 10**6,
        scratch=[pltpu.VMEM(shocks.shape, F32), pltpu.SemaphoreType.DMA],
        limit=8,
    )(lines, block, shocks)
    came, block = lax.optimization_barrier((came, block))
    block = jnp.concatenate([block, came])
    for o in reversed(far[:-1]):
        block = jnp.concatenate([block, swap(block, o)])
    blocks = [block] + [swap(block, o) for o in SQUARE]

    def returns(year, first, width, blocks, xs, before=(), final=True):
        total = secs * sum(b.shape[0] for b in blocks)
        return call(
            functools.partial(returns_body, year, first, secs, len(before) > 0, final),
            [shaped(funds, width), shaped(8, funds)],
            [VMEM] * (len(blocks) + len(before) + 1),
            "returns",
            scratch=[pltpu.VMEM((total, funds), BF16)] * 2
            + [pltpu.VMEM((total, funds), F32)]
            + [pltpu.VMEM((funds, total), BF16)] * 2,
            limit=8 * max(1, min(6, total // 512)),
        )(*blocks, *before, xs)

    before = ()
    for b in blocks[:-1]:
        before = returns(0, 0, paths, [b], x_now, before, False)
    firsts = [returns(0, h * half, half, blocks[-1:], x_now, before) for h in range(2)]
    sums = firsts[0][1]
    part = [p for p, _ in firsts]
    peer = [swap(p, 1) for p in part]
    other_sums = swap(sums, 1)

    later = {0: (part, peer)}
    others = []
    rates = [[None, None] for _ in range(years)]
    final = []

    def advance_half(h):
        first = h * half
        head, state = [sums, other_sums], []
        other = yield sums
        for year in range(years):
            last = year + 1 == years
            pair = [v[h] for v in later[0]] if year == 0 else list(later[year])
            ins = [me_ref] + tie(head, other) + pair + [draws, member, wides] + state
            specs = [SMEM] + [VMEM] * (len(ins) - 1)
            scratch = [pltpu.VMEM((funds, half), F32)]
            if last and h:
                tiles = half // STEP
                out = [shaped(count, paths), shaped(count, paths), shaped(years, owned, funds)]
                out_specs = [ANY, ANY, VMEM]
                scratch += [pltpu.VMEM((tiles, count, STEP), F32)] * 2
                scratch += [pltpu.SemaphoreType.DMA((2, 1 + tiles))]
                before = final[:2] + [v for rs in rates for v in rs if v is not None]
                ins += before
                specs += [VMEM] * len(before)
            elif last:
                out = [shaped(count, half), shaped(count, half), shaped(owned, funds)]
                out_specs = [VMEM] * 3
            else:
                ins.append(member_t)
                specs.append(VMEM)
                out = [shaped(count, half)] * 2
                out += [shaped(2, 2, 2, slice_funds, half), shaped(owned, funds)]
                out_specs = [VMEM] * 4
                scratch += [pltpu.VMEM((2, funds, half), F32)]
            result = call(
                functools.partial(year_body, year, first, last, slice_funds),
                out,
                specs,
                "year",
                flops=2 * 2 * count * 2 * funds * half,
                moved=20 * count * half,
                scratch=scratch,
                out_specs=out_specs,
                limit=10,
            )(*ins)
            if last:
                final[:] = result
                rates[year][h] = result[2]
                yield result[2]
                return
            state, share, rates[year][h] = list(result[:2]), result[2], result[3]
            other = yield share
            held = share[0] + tie(swap(share[1], 1), other)
            if year == 0 and h == 0:
                others.extend(swap(b, 1) for b in tie(blocks, held))
            other = yield held
            held = held[0] + tie(swap(held[1], *FIRST), other)
            other = yield held
            *steps, closing = list(FULL) + [(o,) for o in far[1:]]
            for i, step in enumerate(steps):
                held = held + tie(swap(held, *step), other)
                if i == 0 and h == 0:
                    xs = tie(x_later, held)
                    later[year + 1] = [
                        returns(year + 1, 0, paths, b, xs)[0] for b in (blocks, others)
                    ]
                other = yield held
            own = call(
                functools.partial(own_body, slice_funds, first),
                shaped(slice_funds, half),
                [SMEM] + [VMEM] * 4,
                "own",
                10**6,
                10**6,
                limit=2,
            )(me_ref, *later[year + 1], held, tie(swap(held, *closing), other))
            other = yield own
            near = tie(swap(own, *FIRST), other)
            other = yield near
            head = [own, near, swap(own, 1), swap(near, 1)]

    running = [advance_half(h) for h in range(2)]
    newest = [next(r) for r in running]
    while running:
        for h, r in enumerate(list(running)):
            try:
                newest[h] = r.send(newest[1 - h])
            except StopIteration:
                running.remove(r)
    assets, liability, credit = final
    return assets, liability, credit.transpose(0, 2, 1)


def solution(mesh):
    in_specs = (
        P("grp", None, None),
        P("pol", None),
        P("pol"),
        P("pol", None),
        P("pol", None),
        P("pol"),
        P("pol"),
        P("pol"),
        P("pol"),
        P(),
        P(),
        P("pol", "grp", None),
    )
    out_specs = (P("pol", "grp"), P("pol", "grp"), P("grp", None, "pol"))
    return jax.shard_map(local, mesh=mesh, in_specs=in_specs, out_specs=out_specs, check_vma=False)
```

```python
import functools

import jax
import jax.numpy as jnp
from jax import lax
from jax.experimental import pallas as pl
from jax.experimental.pallas import tpu as pltpu
from jax.sharding import PartitionSpec as P

F32, BF16 = jnp.float32, jnp.bfloat16
SQUARE = (2, 4, 6)
FIRST = (2, 4)
FULL = ((4, 8), (8, 2))
VMEM = pl.BlockSpec(memory_space=pltpu.VMEM)
SMEM = pl.BlockSpec(memory_space=pltpu.SMEM)
ANY = pl.BlockSpec(memory_space=pl.ANY)
HBM = pl.BlockSpec(memory_space=pltpu.HBM)
ROW = (((1,), (1,)), ((), ()))


def swap(x, offset, odd=None):
    n = lax.axis_size("pol")
    offsets = (offset, offset if odd is None else odd)
    return lax.ppermute(x, "pol", [(i, i ^ offsets[i % 2]) for i in range(n)])


def tie(x, other):
    return lax.optimization_barrier((x, other))[0]


def far_offsets():
    n = lax.axis_size("pol")
    return [1 << b for b in range(3, n.bit_length() - 1)]


def rate(ratio):
    x = 20.0 * (ratio - 1.05)
    return 0.01 + (jnp.maximum(x, 0.0) + jnp.log1p(jnp.exp(-jnp.abs(x)))) / 20.0


def halves(v):
    hi = v.astype(BF16)
    return hi, (v - hi.astype(F32)).astype(BF16)


def dot(a, b, dims=(((1,), (0,)), ((), ()))):
    return lax.dot_general(a, b, dims, preferred_element_type=F32)


def call(body, out, ins, name, flops=0, moved=0, scratch=(), out_specs=None, limit=24):
    return pl.pallas_call(
        body,
        out_shape=out,
        in_specs=ins,
        out_specs=out_specs if out_specs is not None else jax.tree.map(lambda _: VMEM, out),
        scratch_shapes=scratch,
        compiler_params=pltpu.CompilerParams(vmem_limit_bytes=int(limit * 2**20)),
        cost_estimate=pl.CostEstimate(flops=flops, bytes_accessed=moved, transcendentals=0),
        name=name,
    )


def shaped(*dims, dtype=F32):
    return jax.ShapeDtypeStruct(dims, dtype)


def pack_body(*refs):
    sources, (out, lines), held, sem = refs[1:11], refs[11:13], refs[13:23], refs[23]
    copies = [pltpu.make_async_copy(s, h, sem.at[i]) for i, (s, h) in enumerate(zip(sources, held))]
    for copy in copies:
        copy.start()
    for copy in copies:
        copy.wait()
    load, hold, drift, fund, term, asset, liab, kind, base, guar = held
    secs, funds = load.shape
    count = fund.shape[1]
    out[0:secs, :] = load[...]
    out[secs : 2 * secs, :] = hold[...]
    member = (lax.broadcasted_iota(jnp.int32, (funds, count), 0) == fund[...]).astype(BF16)
    at = lax.broadcasted_iota(jnp.int32, (8, count), 0)
    alive = (term[...] > 0).astype(F32)
    v = jnp.where(at < 3, asset[...] * alive, liab[...])
    one, rest = v.astype(BF16).astype(F32), v - v.astype(BF16).astype(F32)
    two = rest.astype(BF16).astype(F32)
    three = rest - two
    spot = jnp.where(at < 3, at, at - 3)
    rows = jnp.where(spot == 0, one, jnp.where(spot == 1, two, three))
    rows = jnp.where(at < 6, rows, 0.0).astype(BF16)
    out[2 * secs : 2 * secs + 8, :] = dot(rows, member, ROW)
    fixed = jnp.dot(
        jnp.broadcast_to(drift[...], (8, secs)), hold[...], precision=lax.Precision.HIGHEST
    )
    out[2 * secs + 6 : 2 * secs + 7, :] = fixed[0:1, :]
    base_row = jnp.zeros((1, count), F32)
    guar_row = jnp.zeros((1, count), F32)
    for t in range(base.shape[1]):
        base_row = jnp.where(kind[...] == t, base[:, t : t + 1], base_row)
        guar_row = jnp.where(kind[...] == t, guar[:, t : t + 1], guar_row)
    values = (fund[...].astype(F32), term[...].astype(F32), base_row, guar_row, asset[...], liab[...])
    stack = jnp.zeros((8, count), F32)
    for r, row in enumerate(values):
        stack = jnp.where(at == r, row, stack)
    lines[...] = stack


def columns_body(lines, block, shocks, member_t, member, wides, x_now, x_later, own, raw, sem):
    own[0] = block[...]
    years, funds, count = member_t.shape
    fetch = pltpu.make_async_copy(shocks, raw, sem)
    fetch.start()
    stack = jnp.concatenate([lines[...], jnp.zeros((120, count), F32)], 0)
    cols = jnp.transpose(stack)
    wide = lambda r: jnp.broadcast_to(cols[:, r : r + 1], (count, 128))
    fund_c, term_c, base_c, guar_c = wide(0), wide(1), wide(2), wide(3)
    wides[2 * years] = wide(4)
    wides[2 * years + 1] = wide(5)
    hot_t = lax.broadcasted_iota(jnp.int32, (funds, count), 0).astype(F32) == lines[0:1, :]
    hot = lax.broadcasted_iota(jnp.int32, (count, funds), 1).astype(F32) == fund_c
    for y in range(years):
        alive = term_c > float(y)
        wides[2 * y] = jnp.where(alive, base_c, 0.0)
        wides[2 * y + 1] = jnp.where(alive, guar_c, 0.0)
        here = jnp.logical_and(hot, alive).astype(F32).astype(BF16)
        member[y, :, 0:funds] = here
        member[y, :, funds : 2 * funds] = here
        if y == 0:
            member_t[y] = hot_t.astype(F32).astype(BF16)
        else:
            member_t[y] = jnp.logical_and(hot_t, lines[1:2, :] > float(y)).astype(F32).astype(BF16)
    fetch.wait()
    for y in range(years):
        hi, lo = halves(raw[y])
        if y == 0:
            x_now[0], x_now[1] = hi, lo
        else:
            x_later[y - 1, 0], x_later[y - 1, 1] = hi, lo


def returns_body(year, first, secs, begun, final, *refs):
    *blocks, xs, part, sums, load_hi, load_lo, held, flip_hi, flip_lo = refs
    if begun:
        *blocks, before, sums_before = blocks
    funds, width = part.shape
    total = load_hi.shape[0]
    at = 0
    extra = sums_before[...] if begun else jnp.zeros((8, funds), F32)
    for block in blocks:
        for b in range(block.shape[0]):
            load_hi[at : at + secs, :], load_lo[at : at + secs, :] = halves(block[b, 0:secs, :])
            held[at : at + secs, :] = block[b, secs : 2 * secs, :]
            extra = extra + block[b, 2 * secs : 2 * secs + 8, :]
            at += secs
    sums[...] = extra
    for g in range(0, total, 128):
        flip_hi[:, g : g + 128], flip_lo[:, g : g + 128] = halves(jnp.transpose(held[g : g + 128, :]))
    if final:
        row = lax.broadcasted_iota(jnp.int32, (128, funds), 0)
        fixed = jnp.transpose(jnp.where(row == 0, extra[6:7, :], 0.0))[:, 0:1]
    step = min(256, width)
    group = min(512, total)

    def exposed(c, g):
        cut = slice(first + c, first + c + step)
        x_hi, x_lo = (xs[i, :, cut] if year == 0 else xs[year - 1, i, :, cut] for i in range(2))
        lh, ll = load_hi[g : g + group, :], load_lo[g : g + group, :]
        return dot(jnp.concatenate([lh, lh], 1), jnp.concatenate([x_hi, x_lo], 0)) + dot(ll, x_hi)

    spots = [(c, g) for c in range(0, width, step) for g in range(0, total, group)]
    ahead = exposed(*spots[0])
    for i, (c, g) in enumerate(spots):
        now = ahead
        ahead = exposed(*spots[i + 1]) if i + 1 < len(spots) else None
        t_hi, t_lo = halves(jnp.tanh(now))
        fh, fl = flip_hi[:, g : g + group], flip_lo[:, g : g + group]
        new = 0.25 * dot(jnp.concatenate([fh, fh, fl], 1), jnp.concatenate([t_hi, t_lo, t_hi], 0))
        acc = new if g == 0 else acc + new
        if g + group == total:
            if begun:
                acc = acc + before[:, first + c : first + c + step]
            part[:, c : c + step] = acc + fixed if final else acc


def own_columns(me_ref, declared, first, out):
    paths, funds = out.shape
    width = declared.shape[1]
    spot = lax.broadcasted_iota(jnp.int32, (paths, width), 1) + first
    pick = spot == lax.broadcasted_iota(jnp.int32, (paths, width), 0) + me_ref[0] * paths
    pick = pick.astype(F32).astype(BF16)
    one, rest = declared.astype(BF16), declared - declared.astype(BF16).astype(F32)
    two, three = halves(rest)
    out[...] = dot(pick, one, ROW) + dot(pick, two, ROW) + dot(pick, three, ROW)


def slice_spot(me, order, slice_funds):
    core = (me & 1) ^ (order >> 1)
    side = ((me >> (1 + core)) & 1) ^ (order & 1)
    return pl.multiple_of((2 * core + side) * slice_funds, slice_funds)


def advance(step, got, base, guar, draw, asset, liab):
    wide = lambda v: jnp.concatenate([v] * (step // 128), 1)
    growth, credit = got[:, 0:step], jnp.maximum(got[:, step:], wide(guar))
    lapse = jnp.minimum(wide(base) * (0.5 + draw.astype(F32)) * jnp.exp(5.0 * (growth - credit)), 0.5)
    stay = 1.0 - lapse
    return asset * (1.0 + growth) * stay, liab * (1.0 + credit) * stay


def table_of(growth, declared):
    g_hi, g_lo = halves(growth)
    d_hi, d_lo = halves(declared)
    return jnp.concatenate([jnp.concatenate([g_hi, d_hi], 1), jnp.concatenate([g_lo, d_lo], 1)], 0)


def own_body(slice_funds, first, me, part, peer, *refs):
    totals, out = refs[:-1], refs[-1]
    rows = pl.ds(slice_spot(me[0], 0, slice_funds), slice_funds)
    cut = slice(first, first + out.shape[1])
    growth = part[rows, cut] + peer[rows, cut]
    asset, liab = totals[0][0], totals[0][1]
    for t in totals[1:]:
        asset, liab = asset + t[0], liab + t[1]
    out[...] = rate(asset * (1.0 + growth) / liab)


STEP, ROWS = 256, 512


def year_body(year, first, last, slice_funds, *refs):
    refs = list(refs)
    me = refs.pop(0)
    if year == 0:
        mine, other = refs.pop(0), refs.pop(0)
    else:
        slices = [refs.pop(0) for _ in range(4)]
    part, peer = refs.pop(0), refs.pop(0)
    draws, member, wides = refs.pop(0), refs.pop(0), refs.pop(0)
    held = [refs.pop(0) for _ in range(2 if year else 0)]
    lead = 0
    copies = []
    if last and first:
        half_a, half_l, *earlier, out_a, out_l, out_r, declared, buf_a, buf_l, sem = refs
        own = out_r.at[year]
        for k, (half, out) in enumerate(((half_a, out_a), (half_l, out_l))):
            copies.append(pltpu.make_async_copy(half, out.at[:, 0:first], sem.at[k, 0]))
            copies[-1].start()
    elif last:
        out_a, out_l, own, declared = refs
    else:
        member_t = refs.pop(0)
        out_a, out_l, out_s, own, declared, acc = refs
    funds, width = declared.shape
    count = member.shape[1]
    if year == 0:
        sums = mine[...] + other[...]
        row = lax.broadcasted_iota(jnp.int32, (128, funds), 0)
        start_a = sums[0:1, :] + sums[1:2, :] + sums[2:3, :]
        start_l = sums[3:4, :] + sums[4:5, :] + sums[5:6, :]
        both = jnp.where(row == 0, start_a, jnp.where(row == 1, start_l, 0.0))
        both = jnp.transpose(both)
        ratio = both[:, 0:1] / both[:, 1:2]
        declared[...] = rate(ratio * (1.0 + (part[...] + peer[...])))
    else:
        lead = first
        for o in range(4):
            declared[pl.ds(slice_spot(me[0], o, slice_funds), slice_funds), :] = slices[o][...]
    if last and first:
        for y in range(year):
            out_r[y] = earlier[2 * y][...] + earlier[2 * y + 1][...]

    def gathered(c):
        there = slice(lead + c, lead + c + STEP)
        table = table_of(part[:, there] + peer[:, there], declared[:, c : c + STEP])
        return [dot(member[year, r : r + ROWS, :], table) for r in range(0, count, ROWS)]

    ahead = gathered(0)
    for c in range(0, width, STEP):
        cut = slice(c, c + STEP)
        now = ahead
        ahead = gathered(c + STEP) if c + STEP < width else None
        sum_a = sum_l = None
        for r in range(0, count, ROWS):
            rows = slice(r, r + ROWS)
            if year == 0:
                years = member.shape[0]
                asset = jnp.concatenate([wides[2 * years, rows, :]] * (STEP // 128), 1)
                liab = jnp.concatenate([wides[2 * years + 1, rows, :]] * (STEP // 128), 1)
            else:
                asset, liab = held[0][rows, cut], held[1][rows, cut]
            asset, liab = advance(
                STEP, now[r // ROWS], wides[2 * year, rows, :], wides[2 * year + 1, rows, :],
                draws[year, rows, first + c : first + c + STEP], asset, liab,
            )
            if last and first:
                buf_a[c // STEP, rows, :] = asset
                buf_l[c // STEP, rows, :] = liab
            else:
                out_a[rows, cut] = asset
                out_l[rows, cut] = liab
            if not last:
                a_hi, a_lo = halves(asset)
                l_hi, l_lo = halves(liab)
                ma, ml = member_t[year + 1, :, rows], member_t[0, :, rows]
                add_a = dot(jnp.concatenate([ma, ma], 1), jnp.concatenate([a_hi, a_lo], 0))
                add_l = dot(jnp.concatenate([ml, ml], 1), jnp.concatenate([l_hi, l_lo], 0))
                sum_a = add_a if sum_a is None else sum_a + add_a
                sum_l = add_l if sum_l is None else sum_l + add_l
        if last and first:
            for buf, out, k in ((buf_a, out_a, 0), (buf_l, out_l, 1)):
                copy = pltpu.make_async_copy(
                    buf.at[c // STEP], out.at[:, first + c : first + c + STEP], sem.at[k, 1 + c // STEP]
                )
                copy.start()
                copies.append(copy)
        elif not last:
            acc[0, :, cut] = sum_a
            acc[1, :, cut] = sum_l
    own_columns(me, declared[...], first, own)
    if last and first:
        out_r[year] = out_r[year] + earlier[2 * year][...]
    for copy in copies:
        copy.wait()
    if not last:
        for o in range(4):
            for v in range(2):
                spot = pl.ds(slice_spot(me[0], o, slice_funds), slice_funds)
                out_s[o // 2, o % 2, v] = acc[v, spot, :]


def local(
    shocks,
    loadings,
    sec_drift,
    holdings,
    fund_of,
    product_type,
    term_years,
    asset_start,
    liab_start,
    base_lapse,
    guarantee,
    lapse_draw,
):
    years, _, paths = shocks.shape
    secs, funds = holdings.shape
    count = asset_start.shape[0]
    n = lax.axis_size("pol")
    me = lax.axis_index("pol")
    me_ref = me.astype(jnp.int32).reshape(1)
    slice_funds = funds // 4
    owned = paths // n
    half = paths // 2
    draws = lapse_draw.transpose(1, 0, 2)
    line = lambda v: v.reshape(1, count)
    fund, kind, term = line(fund_of), line(product_type), line(term_years)
    asset, liab = line(asset_start), line(liab_start)

    sources = [loadings, holdings, sec_drift.reshape(1, secs), fund, term, asset, liab, kind]
    sources += [base_lapse.reshape(1, -1), guarantee.reshape(1, -1)]
    block, lines = call(
        pack_body,
        [shaped(2 * secs + 8, funds), shaped(8, count)],
        [SMEM] + [HBM] * 10,
        "pack",
        10**6,
        10**5,
        scratch=[pltpu.VMEM(v.shape, v.dtype) for v in sources] + [pltpu.SemaphoreType.DMA((10,))],
        limit=60,
    )(me_ref, *sources)
    far = far_offsets()
    came = swap(block[None], far[-1])
    member_t, member, wides, x_now, x_later, block = call(
        columns_body,
        [
            shaped(years, funds, count, dtype=BF16),
            shaped(years, count, 2 * funds, dtype=BF16),
            shaped(2 * years + 2, count, 128),
            shaped(2, *shocks.shape[1:], dtype=BF16),
            shaped(years - 1, 2, *shocks.shape[1:], dtype=BF16),
            shaped(1, *block.shape),
        ],
        [VMEM, VMEM, HBM],
        "columns",
        10**6,
        4 * 10**6,
        scratch=[pltpu.VMEM(shocks.shape, F32), pltpu.SemaphoreType.DMA],
        limit=8,
    )(lines, block, shocks)
    came, block = lax.optimization_barrier((came, block))
    block = jnp.concatenate([block, came])
    for o in reversed(far[:-1]):
        block = jnp.concatenate([block, swap(block, o)])
    blocks = [block] + [swap(block, o) for o in SQUARE]

    def returns(year, first, width, blocks, xs, before=(), final=True):
        total = secs * sum(b.shape[0] for b in blocks)
        return call(
            functools.partial(returns_body, year, first, secs, len(before) > 0, final),
            [shaped(funds, width), shaped(8, funds)],
            [VMEM] * (len(blocks) + len(before) + 1),
            "returns",
            scratch=[pltpu.VMEM((total, funds), BF16)] * 2
            + [pltpu.VMEM((total, funds), F32)]
            + [pltpu.VMEM((funds, total), BF16)] * 2,
            limit=8 * max(1, min(6, total // 512)),
        )(*blocks, *before, xs)

    before = ()
    for b in blocks[:-1]:
        before = returns(0, 0, paths, [b], x_now, before, False)
    firsts = [returns(0, h * half, half, blocks[-1:], x_now, before) for h in range(2)]
    sums = firsts[0][1]
    part = [p for p, _ in firsts]
    peer = [swap(p, 1) for p in part]
    other_sums = swap(sums, 1)

    later = {0: (part, peer)}
    others = []
    rates = [[None, None] for _ in range(years)]
    final = []

    def advance_half(h):
        first = h * half
        head, state = [sums, other_sums], []
        other = yield sums
        for year in range(years):
            last = year + 1 == years
            pair = [v[h] for v in later[0]] if year == 0 else list(later[year])
            ins = [me_ref] + tie(head, other) + pair + [draws, member, wides] + state
            specs = [SMEM] + [VMEM] * (len(ins) - 1)
            scratch = [pltpu.VMEM((funds, half), F32)]
            if last and h:
                tiles = half // STEP
                out = [shaped(count, paths), shaped(count, paths), shaped(years, owned, funds)]
                out_specs = [ANY, ANY, VMEM]
                scratch += [pltpu.VMEM((tiles, count, STEP), F32)] * 2
                scratch += [pltpu.SemaphoreType.DMA((2, 1 + tiles))]
                before = final[:2] + [v for rs in rates for v in rs if v is not None]
                ins += before
                specs += [VMEM] * len(before)
            elif last:
                out = [shaped(count, half), shaped(count, half), shaped(owned, funds)]
                out_specs = [VMEM] * 3
            else:
                ins.append(member_t)
                specs.append(VMEM)
                out = [shaped(count, half)] * 2
                out += [shaped(2, 2, 2, slice_funds, half), shaped(owned, funds)]
                out_specs = [VMEM] * 4
                scratch += [pltpu.VMEM((2, funds, half), F32)]
            result = call(
                functools.partial(year_body, year, first, last, slice_funds),
                out,
                specs,
                "year",
                flops=2 * 2 * count * 2 * funds * half,
                moved=20 * count * half,
                scratch=scratch,
                out_specs=out_specs,
                limit=10,
            )(*ins)
            if last:
                final[:] = result
                rates[year][h] = result[2]
                yield result[2]
                return
            state, share, rates[year][h] = list(result[:2]), result[2], result[3]
            if year == 0 and h == 1:
                others.append(swap(jnp.concatenate(tie(blocks, share)), 1))
            other = yield share
            held = share[0] + tie(swap(share[1], 1), other)
            other = yield held
            came = tie(swap(held[1], *FIRST), other)
            if h == 0:
                made = returns(year + 1, 0, paths, blocks, tie(x_later, held))[0]
                came, made, ready = lax.optimization_barrier((came, made, list(others)))
                later[year + 1] = [made]
            held = held[0] + came
            other = yield held
            *steps, closing = list(FULL) + [(o,) for o in far[1:]]
            for i, step in enumerate(steps):
                came = tie(swap(held, *step), other)
                if i == 0 and h == 0:
                    made = returns(year + 1, 0, paths, ready, tie(x_later, held))[0]
                    came, made = lax.optimization_barrier((came, made))
                    later[year + 1].append(made)
                held = held + came
                other = yield held
            own = call(
                functools.partial(own_body, slice_funds, first),
                shaped(slice_funds, half),
                [SMEM] + [VMEM] * 4,
                "own",
                10**6,
                10**6,
                limit=2,
            )(me_ref, *later[year + 1], held, tie(swap(held, *closing), other))
            other = yield own
            near = tie(swap(own, *FIRST), other)
            other = yield near
            head = [own, near, swap(own, 1), swap(near, 1)]

    running = [advance_half(h) for h in range(2)]
    newest = [next(r) for r in running]
    while running:
        for h, r in enumerate(list(running)):
            try:
                newest[h] = r.send(newest[1 - h])
            except StopIteration:
                running.remove(r)
    assets, liability, credit = final
    return assets, liability, credit.transpose(0, 2, 1)


def solution(mesh):
    in_specs = (
        P("grp", None, None),
        P("pol", None),
        P("pol"),
        P("pol", None),
        P("pol", None),
        P("pol"),
        P("pol"),
        P("pol"),
        P("pol"),
        P(),
        P(),
        P("pol", "grp", None),
    )
    out_specs = (P("pol", "grp"), P("pol", "grp"), P("grp", None, "pol"))
    return jax.shard_map(local, mesh=mesh, in_specs=in_specs, out_specs=out_specs, check_vma=False)
```

```python
import functools

import jax
import jax.numpy as jnp
from jax import lax
from jax.experimental import pallas as pl
from jax.experimental.pallas import tpu as pltpu
from jax.sharding import PartitionSpec as P

F32, BF16 = jnp.float32, jnp.bfloat16
SQUARE = (2, 4, 6)
FIRST = (2, 4)
FULL = ((4, 8), (8, 2))
VMEM = pl.BlockSpec(memory_space=pltpu.VMEM)
SMEM = pl.BlockSpec(memory_space=pltpu.SMEM)
ANY = pl.BlockSpec(memory_space=pl.ANY)
HBM = pl.BlockSpec(memory_space=pltpu.HBM)
ROW = (((1,), (1,)), ((), ()))


def swap(x, offset, odd=None):
    n = lax.axis_size("pol")
    offsets = (offset, offset if odd is None else odd)
    return lax.ppermute(x, "pol", [(i, i ^ offsets[i % 2]) for i in range(n)])


def tie(x, other):
    return lax.optimization_barrier((x, other))[0]


def far_offsets():
    n = lax.axis_size("pol")
    return [1 << b for b in range(3, n.bit_length() - 1)]


def rate(ratio):
    x = 20.0 * (ratio - 1.05)
    return 0.01 + (jnp.maximum(x, 0.0) + jnp.log1p(jnp.exp(-jnp.abs(x)))) / 20.0


def halves(v):
    hi = v.astype(BF16)
    return hi, (v - hi.astype(F32)).astype(BF16)


def dot(a, b, dims=(((1,), (0,)), ((), ()))):
    return lax.dot_general(a, b, dims, preferred_element_type=F32)


def call(body, out, ins, name, flops=0, moved=0, scratch=(), out_specs=None, limit=24):
    return pl.pallas_call(
        body,
        out_shape=out,
        in_specs=ins,
        out_specs=out_specs if out_specs is not None else jax.tree.map(lambda _: VMEM, out),
        scratch_shapes=scratch,
        compiler_params=pltpu.CompilerParams(vmem_limit_bytes=int(limit * 2**20)),
        cost_estimate=pl.CostEstimate(flops=flops, bytes_accessed=moved, transcendentals=0),
        name=name,
    )


def shaped(*dims, dtype=F32):
    return jax.ShapeDtypeStruct(dims, dtype)


def pack_body(*refs):
    sources, (out, lines), held, sem = refs[1:11], refs[11:13], refs[13:23], refs[23]
    copies = [pltpu.make_async_copy(s, h, sem.at[i]) for i, (s, h) in enumerate(zip(sources, held))]
    for copy in copies:
        copy.start()
    for copy in copies:
        copy.wait()
    load, hold, drift, fund, term, asset, liab, kind, base, guar = held
    secs, funds = load.shape
    count = fund.shape[1]
    out[0:secs, :] = load[...]
    out[secs : 2 * secs, :] = hold[...]
    member = (lax.broadcasted_iota(jnp.int32, (funds, count), 0) == fund[...]).astype(BF16)
    at = lax.broadcasted_iota(jnp.int32, (8, count), 0)
    alive = (term[...] > 0).astype(F32)
    v = jnp.where(at < 3, asset[...] * alive, liab[...])
    one, rest = v.astype(BF16).astype(F32), v - v.astype(BF16).astype(F32)
    two = rest.astype(BF16).astype(F32)
    three = rest - two
    spot = jnp.where(at < 3, at, at - 3)
    rows = jnp.where(spot == 0, one, jnp.where(spot == 1, two, three))
    rows = jnp.where(at < 6, rows, 0.0).astype(BF16)
    out[2 * secs : 2 * secs + 8, :] = dot(rows, member, ROW)
    fixed = jnp.dot(
        jnp.broadcast_to(drift[...], (8, secs)), hold[...], precision=lax.Precision.HIGHEST
    )
    out[2 * secs + 6 : 2 * secs + 7, :] = fixed[0:1, :]
    base_row = jnp.zeros((1, count), F32)
    guar_row = jnp.zeros((1, count), F32)
    for t in range(base.shape[1]):
        base_row = jnp.where(kind[...] == t, base[:, t : t + 1], base_row)
        guar_row = jnp.where(kind[...] == t, guar[:, t : t + 1], guar_row)
    values = (fund[...].astype(F32), term[...].astype(F32), base_row, guar_row, asset[...], liab[...])
    stack = jnp.zeros((8, count), F32)
    for r, row in enumerate(values):
        stack = jnp.where(at == r, row, stack)
    lines[...] = stack


def columns_body(lines, block, shocks, member_t, member, wides, x_now, x_later, own, raw, sem):
    own[0] = block[...]
    years, funds, count = member_t.shape
    fetch = pltpu.make_async_copy(shocks, raw, sem)
    fetch.start()
    stack = jnp.concatenate([lines[...], jnp.zeros((120, count), F32)], 0)
    cols = jnp.transpose(stack)
    wide = lambda r: jnp.broadcast_to(cols[:, r : r + 1], (count, 128))
    fund_c, term_c, base_c, guar_c = wide(0), wide(1), wide(2), wide(3)
    wides[2 * years] = wide(4)
    wides[2 * years + 1] = wide(5)
    hot_t = lax.broadcasted_iota(jnp.int32, (funds, count), 0).astype(F32) == lines[0:1, :]
    hot = lax.broadcasted_iota(jnp.int32, (count, funds), 1).astype(F32) == fund_c
    for y in range(years):
        alive = term_c > float(y)
        wides[2 * y] = jnp.where(alive, base_c, 0.0)
        wides[2 * y + 1] = jnp.where(alive, guar_c, 0.0)
        here = jnp.logical_and(hot, alive).astype(F32).astype(BF16)
        member[y, :, 0:funds] = here
        member[y, :, funds : 2 * funds] = here
        if y == 0:
            member_t[y] = hot_t.astype(F32).astype(BF16)
        else:
            member_t[y] = jnp.logical_and(hot_t, lines[1:2, :] > float(y)).astype(F32).astype(BF16)
    fetch.wait()
    for y in range(years):
        hi, lo = halves(raw[y])
        if y == 0:
            x_now[0], x_now[1] = hi, lo
        else:
            x_later[y - 1, 0], x_later[y - 1, 1] = hi, lo


def returns_body(year, first, secs, begun, final, *refs):
    *blocks, xs, part, sums, load_hi, load_lo, held, flip_hi, flip_lo = refs
    if begun:
        *blocks, before, sums_before = blocks
    funds, width = part.shape
    total = load_hi.shape[0]
    at = 0
    extra = sums_before[...] if begun else jnp.zeros((8, funds), F32)
    for block in blocks:
        for b in range(block.shape[0]):
            load_hi[at : at + secs, :], load_lo[at : at + secs, :] = halves(block[b, 0:secs, :])
            held[at : at + secs, :] = block[b, secs : 2 * secs, :]
            extra = extra + block[b, 2 * secs : 2 * secs + 8, :]
            at += secs
    sums[...] = extra
    for g in range(0, total, 128):
        flip_hi[:, g : g + 128], flip_lo[:, g : g + 128] = halves(jnp.transpose(held[g : g + 128, :]))
    if final:
        row = lax.broadcasted_iota(jnp.int32, (128, funds), 0)
        fixed = jnp.transpose(jnp.where(row == 0, extra[6:7, :], 0.0))[:, 0:1]
    step = min(256, width)
    group = min(512, total)

    def exposed(c, g):
        cut = slice(first + c, first + c + step)
        x_hi, x_lo = (xs[i, :, cut] if year == 0 else xs[year - 1, i, :, cut] for i in range(2))
        lh, ll = load_hi[g : g + group, :], load_lo[g : g + group, :]
        return dot(jnp.concatenate([lh, lh], 1), jnp.concatenate([x_hi, x_lo], 0)) + dot(ll, x_hi)

    spots = [(c, g) for c in range(0, width, step) for g in range(0, total, group)]
    ahead = exposed(*spots[0])
    for i, (c, g) in enumerate(spots):
        now = ahead
        ahead = exposed(*spots[i + 1]) if i + 1 < len(spots) else None
        t_hi, t_lo = halves(jnp.tanh(now))
        fh, fl = flip_hi[:, g : g + group], flip_lo[:, g : g + group]
        new = 0.25 * dot(jnp.concatenate([fh, fh, fl], 1), jnp.concatenate([t_hi, t_lo, t_hi], 0))
        acc = new if g == 0 else acc + new
        if g + group == total:
            if begun:
                acc = acc + before[:, first + c : first + c + step]
            part[:, c : c + step] = acc + fixed if final else acc


def own_columns(me_ref, declared, first, out):
    paths, funds = out.shape
    width = declared.shape[1]
    spot = lax.broadcasted_iota(jnp.int32, (paths, width), 1) + first
    pick = spot == lax.broadcasted_iota(jnp.int32, (paths, width), 0) + me_ref[0] * paths
    pick = pick.astype(F32).astype(BF16)
    one, rest = declared.astype(BF16), declared - declared.astype(BF16).astype(F32)
    two, three = halves(rest)
    out[...] = dot(pick, one, ROW) + dot(pick, two, ROW) + dot(pick, three, ROW)


def slice_spot(me, order, slice_funds):
    core = (me & 1) ^ (order >> 1)
    side = ((me >> (1 + core)) & 1) ^ (order & 1)
    return pl.multiple_of((2 * core + side) * slice_funds, slice_funds)


def advance(step, got, base, guar, draw, asset, liab):
    wide = lambda v: jnp.concatenate([v] * (step // 128), 1)
    growth, credit = got[:, 0:step], jnp.maximum(got[:, step:], wide(guar))
    lapse = jnp.minimum(wide(base) * (0.5 + draw.astype(F32)) * jnp.exp(5.0 * (growth - credit)), 0.5)
    stay = 1.0 - lapse
    return asset * (1.0 + growth) * stay, liab * (1.0 + credit) * stay


def table_of(growth, declared):
    g_hi, g_lo = halves(growth)
    d_hi, d_lo = halves(declared)
    return jnp.concatenate([jnp.concatenate([g_hi, d_hi], 1), jnp.concatenate([g_lo, d_lo], 1)], 0)


def own_body(slice_funds, first, me, part, peer, *refs):
    totals, out = refs[:-1], refs[-1]
    rows = pl.ds(slice_spot(me[0], 0, slice_funds), slice_funds)
    cut = slice(first, first + out.shape[1])
    growth = part[rows, cut] + peer[rows, cut]
    asset, liab = totals[0][0], totals[0][1]
    for t in totals[1:]:
        asset, liab = asset + t[0], liab + t[1]
    out[...] = rate(asset * (1.0 + growth) / liab)


STEP, ROWS = 256, 512


def year_body(year, first, last, slice_funds, *refs):
    refs = list(refs)
    me = refs.pop(0)
    if year == 0:
        mine, other = refs.pop(0), refs.pop(0)
    else:
        slices = [refs.pop(0) for _ in range(4)]
    part, peer = refs.pop(0), refs.pop(0)
    draws, member, wides = refs.pop(0), refs.pop(0), refs.pop(0)
    held = [refs.pop(0) for _ in range(2 if year else 0)]
    lead = 0
    copies = []
    if last and first:
        half_a, half_l, *earlier, out_a, out_l, out_r, declared, buf_a, buf_l, rates, sem = refs
        for k, (half, out) in enumerate(((half_a, out_a), (half_l, out_l))):
            copies.append(pltpu.make_async_copy(half, out.at[:, 0:first], sem.at[k, 0]))
            copies[-1].start()
    elif last:
        out_a, out_l, own, declared = refs
    else:
        member_t = refs.pop(0)
        out_a, out_l, out_s, own, declared, acc = refs
    funds, width = declared.shape
    count = member.shape[1]
    if year == 0:
        sums = mine[...] + other[...]
        row = lax.broadcasted_iota(jnp.int32, (128, funds), 0)
        start_a = sums[0:1, :] + sums[1:2, :] + sums[2:3, :]
        start_l = sums[3:4, :] + sums[4:5, :] + sums[5:6, :]
        both = jnp.where(row == 0, start_a, jnp.where(row == 1, start_l, 0.0))
        both = jnp.transpose(both)
        ratio = both[:, 0:1] / both[:, 1:2]
        declared[...] = rate(ratio * (1.0 + (part[...] + peer[...])))
    else:
        lead = first
        for o in range(4):
            declared[pl.ds(slice_spot(me[0], o, slice_funds), slice_funds), :] = slices[o][...]
    if last and first:
        own_columns(me, declared[...], first, rates.at[year])
        rates[year] = rates[year] + earlier[2 * year][...]
        for y in range(year):
            rates[y] = earlier[2 * y][...] + earlier[2 * y + 1][...]
        copies.append(pltpu.make_async_copy(rates, out_r, sem.at[2, 0]))
        copies[-1].start()

    def gathered(c):
        there = slice(lead + c, lead + c + STEP)
        table = table_of(part[:, there] + peer[:, there], declared[:, c : c + STEP])
        return [dot(member[year, r : r + ROWS, :], table) for r in range(0, count, ROWS)]

    ahead = gathered(0)
    for c in range(0, width, STEP):
        cut = slice(c, c + STEP)
        now = ahead
        ahead = gathered(c + STEP) if c + STEP < width else None
        sum_a = sum_l = None
        for r in range(0, count, ROWS):
            rows = slice(r, r + ROWS)
            if year == 0:
                years = member.shape[0]
                asset = jnp.concatenate([wides[2 * years, rows, :]] * (STEP // 128), 1)
                liab = jnp.concatenate([wides[2 * years + 1, rows, :]] * (STEP // 128), 1)
            else:
                asset, liab = held[0][rows, cut], held[1][rows, cut]
            asset, liab = advance(
                STEP, now[r // ROWS], wides[2 * year, rows, :], wides[2 * year + 1, rows, :],
                draws[year, rows, first + c : first + c + STEP], asset, liab,
            )
            if last and first:
                buf_a[c // STEP, rows, :] = asset
                buf_l[c // STEP, rows, :] = liab
            else:
                out_a[rows, cut] = asset
                out_l[rows, cut] = liab
            if not last:
                a_hi, a_lo = halves(asset)
                l_hi, l_lo = halves(liab)
                ma, ml = member_t[year + 1, :, rows], member_t[0, :, rows]
                add_a = dot(jnp.concatenate([ma, ma], 1), jnp.concatenate([a_hi, a_lo], 0))
                add_l = dot(jnp.concatenate([ml, ml], 1), jnp.concatenate([l_hi, l_lo], 0))
                sum_a = add_a if sum_a is None else sum_a + add_a
                sum_l = add_l if sum_l is None else sum_l + add_l
        if last and first:
            for buf, out, k in ((buf_a, out_a, 0), (buf_l, out_l, 1)):
                copy = pltpu.make_async_copy(
                    buf.at[c // STEP], out.at[:, first + c : first + c + STEP], sem.at[k, 1 + c // STEP]
                )
                copy.start()
                copies.append(copy)
        elif not last:
            acc[0, :, cut] = sum_a
            acc[1, :, cut] = sum_l
    if not (last and first):
        own_columns(me, declared[...], first, own)
    for copy in copies:
        copy.wait()
    if not last:
        for o in range(4):
            for v in range(2):
                spot = pl.ds(slice_spot(me[0], o, slice_funds), slice_funds)
                out_s[o // 2, o % 2, v] = acc[v, spot, :]


def local(
    shocks,
    loadings,
    sec_drift,
    holdings,
    fund_of,
    product_type,
    term_years,
    asset_start,
    liab_start,
    base_lapse,
    guarantee,
    lapse_draw,
):
    years, _, paths = shocks.shape
    secs, funds = holdings.shape
    count = asset_start.shape[0]
    n = lax.axis_size("pol")
    me = lax.axis_index("pol")
    me_ref = me.astype(jnp.int32).reshape(1)
    slice_funds = funds // 4
    owned = paths // n
    half = paths // 2
    draws = lapse_draw.transpose(1, 0, 2)
    line = lambda v: v.reshape(1, count)
    fund, kind, term = line(fund_of), line(product_type), line(term_years)
    asset, liab = line(asset_start), line(liab_start)

    sources = [loadings, holdings, sec_drift.reshape(1, secs), fund, term, asset, liab, kind]
    sources += [base_lapse.reshape(1, -1), guarantee.reshape(1, -1)]
    block, lines = call(
        pack_body,
        [shaped(2 * secs + 8, funds), shaped(8, count)],
        [SMEM] + [HBM] * 10,
        "pack",
        10**6,
        10**5,
        scratch=[pltpu.VMEM(v.shape, v.dtype) for v in sources] + [pltpu.SemaphoreType.DMA((10,))],
        limit=60,
    )(me_ref, *sources)
    far = far_offsets()
    came = swap(block[None], far[-1])
    member_t, member, wides, x_now, x_later, block = call(
        columns_body,
        [
            shaped(years, funds, count, dtype=BF16),
            shaped(years, count, 2 * funds, dtype=BF16),
            shaped(2 * years + 2, count, 128),
            shaped(2, *shocks.shape[1:], dtype=BF16),
            shaped(years - 1, 2, *shocks.shape[1:], dtype=BF16),
            shaped(1, *block.shape),
        ],
        [VMEM, VMEM, HBM],
        "columns",
        10**6,
        4 * 10**6,
        scratch=[pltpu.VMEM(shocks.shape, F32), pltpu.SemaphoreType.DMA],
        limit=8,
    )(lines, block, shocks)
    came, block = lax.optimization_barrier((came, block))
    block = jnp.concatenate([block, came])
    for o in reversed(far[:-1]):
        block = jnp.concatenate([block, swap(block, o)])
    blocks = [block] + [swap(block, o) for o in SQUARE]

    def returns(year, first, width, blocks, xs, before=(), final=True):
        total = secs * sum(b.shape[0] for b in blocks)
        return call(
            functools.partial(returns_body, year, first, secs, len(before) > 0, final),
            [shaped(funds, width), shaped(8, funds)],
            [VMEM] * (len(blocks) + len(before) + 1),
            "returns",
            scratch=[pltpu.VMEM((total, funds), BF16)] * 2
            + [pltpu.VMEM((total, funds), F32)]
            + [pltpu.VMEM((funds, total), BF16)] * 2,
            limit=8 * max(1, min(6, total // 512)),
        )(*blocks, *before, xs)

    before = ()
    for b in blocks[:-1]:
        before = returns(0, 0, paths, [b], x_now, before, False)
    firsts = [returns(0, h * half, half, blocks[-1:], x_now, before) for h in range(2)]
    sums = firsts[0][1]
    part = [p for p, _ in firsts]
    peer = [swap(p, 1) for p in part]
    other_sums = swap(sums, 1)

    later = {0: (part, peer)}
    others = []
    rates = [[None, None] for _ in range(years)]
    final = []

    def advance_half(h):
        first = h * half
        head, state = [sums, other_sums], []
        other = yield sums
        for year in range(years):
            last = year + 1 == years
            pair = [v[h] for v in later[0]] if year == 0 else list(later[year])
            ins = [me_ref] + tie(head, other) + pair + [draws, member, wides] + state
            specs = [SMEM] + [VMEM] * (len(ins) - 1)
            scratch = [pltpu.VMEM((funds, half), F32)]
            if last and h:
                tiles = half // STEP
                out = [shaped(count, paths), shaped(count, paths), shaped(years, owned, funds)]
                out_specs = [ANY] * 3
                scratch += [pltpu.VMEM((tiles, count, STEP), F32)] * 2
                scratch += [pltpu.VMEM((years, owned, funds), F32)]
                scratch += [pltpu.SemaphoreType.DMA((3, 1 + tiles))]
                before = final[:2] + [v for rs in rates for v in rs if v is not None]
                ins += before
                specs += [VMEM] * len(before)
            elif last:
                out = [shaped(count, half), shaped(count, half), shaped(owned, funds)]
                out_specs = [VMEM] * 3
            else:
                ins.append(member_t)
                specs.append(VMEM)
                out = [shaped(count, half)] * 2
                out += [shaped(2, 2, 2, slice_funds, half), shaped(owned, funds)]
                out_specs = [VMEM] * 4
                scratch += [pltpu.VMEM((2, funds, half), F32)]
            result = call(
                functools.partial(year_body, year, first, last, slice_funds),
                out,
                specs,
                "year",
                flops=2 * 2 * count * 2 * funds * half,
                moved=20 * count * half,
                scratch=scratch,
                out_specs=out_specs,
                limit=10,
            )(*ins)
            if last:
                final[:] = result
                rates[year][h] = result[2]
                yield result[2]
                return
            state, share, rates[year][h] = list(result[:2]), result[2], result[3]
            if year == 0 and h == 1:
                others.append(swap(jnp.concatenate(tie(blocks, share)), 1))
            other = yield share
            held = share[0] + tie(swap(share[1], 1), other)
            other = yield held
            came = tie(swap(held[1], *FIRST), other)
            if h == 0:
                made = returns(year + 1, 0, paths, blocks, tie(x_later, held))[0]
                came, made, ready = lax.optimization_barrier((came, made, list(others)))
                later[year + 1] = [made]
            held = held[0] + came
            other = yield held
            *steps, closing = list(FULL) + [(o,) for o in far[1:]]
            for i, step in enumerate(steps):
                came = tie(swap(held, *step), other)
                if i == 0 and h == 0:
                    made = returns(year + 1, 0, paths, ready, tie(x_later, held))[0]
                    came, made = lax.optimization_barrier((came, made))
                    later[year + 1].append(made)
                held = held + came
                other = yield held
            own = call(
                functools.partial(own_body, slice_funds, first),
                shaped(slice_funds, half),
                [SMEM] + [VMEM] * 4,
                "own",
                10**6,
                10**6,
                limit=2,
            )(me_ref, *later[year + 1], held, tie(swap(held, *closing), other))
            other = yield own
            near = tie(swap(own, *FIRST), other)
            other = yield near
            head = [own, near, swap(own, 1), swap(near, 1)]

    running = [advance_half(h) for h in range(2)]
    newest = [next(r) for r in running]
    while running:
        for h, r in enumerate(list(running)):
            try:
                newest[h] = r.send(newest[1 - h])
            except StopIteration:
                running.remove(r)
    assets, liability, credit = final
    return assets, liability, credit.transpose(0, 2, 1)


def solution(mesh):
    in_specs = (
        P("grp", None, None),
        P("pol", None),
        P("pol"),
        P("pol", None),
        P("pol", None),
        P("pol"),
        P("pol"),
        P("pol"),
        P("pol"),
        P(),
        P(),
        P("pol", "grp", None),
    )
    out_specs = (P("pol", "grp"), P("pol", "grp"), P("grp", None, "pol"))
    return jax.shard_map(local, mesh=mesh, in_specs=in_specs, out_specs=out_specs, check_vma=False)
```

```python
import functools

import jax
import jax.numpy as jnp
from jax import lax
from jax.experimental import pallas as pl
from jax.experimental.pallas import tpu as pltpu
from jax.sharding import PartitionSpec as P

F32, BF16 = jnp.float32, jnp.bfloat16
SQUARE = (2, 4, 6)
FIRST = (2, 4)
FULL = ((4, 8), (8, 2))
VMEM = pl.BlockSpec(memory_space=pltpu.VMEM)
SMEM = pl.BlockSpec(memory_space=pltpu.SMEM)
ANY = pl.BlockSpec(memory_space=pl.ANY)
HBM = pl.BlockSpec(memory_space=pltpu.HBM)
ROW = (((1,), (1,)), ((), ()))


def swap(x, offset, odd=None):
    n = lax.axis_size("pol")
    offsets = (offset, offset if odd is None else odd)
    return lax.ppermute(x, "pol", [(i, i ^ offsets[i % 2]) for i in range(n)])


def tie(x, other):
    return lax.optimization_barrier((x, other))[0]


def far_offsets():
    n = lax.axis_size("pol")
    return [1 << b for b in range(3, n.bit_length() - 1)]


def rate(ratio):
    x = 20.0 * (ratio - 1.05)
    return 0.01 + (jnp.maximum(x, 0.0) + jnp.log1p(jnp.exp(-jnp.abs(x)))) / 20.0


def halves(v):
    hi = v.astype(BF16)
    return hi, (v - hi.astype(F32)).astype(BF16)


def dot(a, b, dims=(((1,), (0,)), ((), ()))):
    return lax.dot_general(a, b, dims, preferred_element_type=F32)


def call(body, out, ins, name, flops=0, moved=0, scratch=(), out_specs=None, limit=24):
    return pl.pallas_call(
        body,
        out_shape=out,
        in_specs=ins,
        out_specs=out_specs if out_specs is not None else jax.tree.map(lambda _: VMEM, out),
        scratch_shapes=scratch,
        compiler_params=pltpu.CompilerParams(vmem_limit_bytes=int(limit * 2**20)),
        cost_estimate=pl.CostEstimate(flops=flops, bytes_accessed=moved, transcendentals=0),
        name=name,
    )


def shaped(*dims, dtype=F32):
    return jax.ShapeDtypeStruct(dims, dtype)


def pack_body(*refs):
    sources, (out, lines), held, sem = refs[1:11], refs[11:13], refs[13:23], refs[23]
    copies = [pltpu.make_async_copy(s, h, sem.at[i]) for i, (s, h) in enumerate(zip(sources, held))]
    for copy in copies:
        copy.start()
    for copy in copies:
        copy.wait()
    load, hold, drift, fund, term, asset, liab, kind, base, guar = held
    secs, funds = load.shape
    count = fund.shape[1]
    out[0:secs, :] = load[...]
    out[secs : 2 * secs, :] = hold[...]
    member = (lax.broadcasted_iota(jnp.int32, (funds, count), 0) == fund[...]).astype(BF16)
    at = lax.broadcasted_iota(jnp.int32, (8, count), 0)
    alive = (term[...] > 0).astype(F32)
    v = jnp.where(at < 3, asset[...] * alive, liab[...])
    one, rest = v.astype(BF16).astype(F32), v - v.astype(BF16).astype(F32)
    two = rest.astype(BF16).astype(F32)
    three = rest - two
    spot = jnp.where(at < 3, at, at - 3)
    rows = jnp.where(spot == 0, one, jnp.where(spot == 1, two, three))
    rows = jnp.where(at < 6, rows, 0.0).astype(BF16)
    out[2 * secs : 2 * secs + 8, :] = dot(rows, member, ROW)
    fixed = jnp.dot(
        jnp.broadcast_to(drift[...], (8, secs)), hold[...], precision=lax.Precision.HIGHEST
    )
    out[2 * secs + 6 : 2 * secs + 7, :] = fixed[0:1, :]
    base_row = jnp.zeros((1, count), F32)
    guar_row = jnp.zeros((1, count), F32)
    for t in range(base.shape[1]):
        base_row = jnp.where(kind[...] == t, base[:, t : t + 1], base_row)
        guar_row = jnp.where(kind[...] == t, guar[:, t : t + 1], guar_row)
    values = (fund[...].astype(F32), term[...].astype(F32), base_row, guar_row, asset[...], liab[...])
    stack = jnp.zeros((8, count), F32)
    for r, row in enumerate(values):
        stack = jnp.where(at == r, row, stack)
    lines[...] = stack


def columns_body(lines, block, shocks, member_t, member, wides, x_now, x_later, own, raw, sem):
    own[0] = block[...]
    years, funds, count = member_t.shape
    fetch = pltpu.make_async_copy(shocks, raw, sem)
    fetch.start()
    stack = jnp.concatenate([lines[...], jnp.zeros((120, count), F32)], 0)
    cols = jnp.transpose(stack)
    wide = lambda r: jnp.broadcast_to(cols[:, r : r + 1], (count, 128))
    fund_c, term_c, base_c, guar_c = wide(0), wide(1), wide(2), wide(3)
    wides[2 * years] = wide(4)
    wides[2 * years + 1] = wide(5)
    hot_t = lax.broadcasted_iota(jnp.int32, (funds, count), 0).astype(F32) == lines[0:1, :]
    hot = lax.broadcasted_iota(jnp.int32, (count, funds), 1).astype(F32) == fund_c
    for y in range(years):
        alive = term_c > float(y)
        wides[2 * y] = jnp.where(alive, base_c, 0.0)
        wides[2 * y + 1] = jnp.where(alive, guar_c, 0.0)
        here = jnp.logical_and(hot, alive).astype(F32).astype(BF16)
        member[y, :, 0:funds] = here
        member[y, :, funds : 2 * funds] = here
        if y == 0:
            member_t[y] = hot_t.astype(F32).astype(BF16)
        else:
            member_t[y] = jnp.logical_and(hot_t, lines[1:2, :] > float(y)).astype(F32).astype(BF16)
    fetch.wait()
    for y in range(years):
        hi, lo = halves(raw[y])
        if y == 0:
            x_now[0], x_now[1] = hi, lo
        else:
            x_later[y - 1, 0], x_later[y - 1, 1] = hi, lo


def returns_body(year, first, secs, begun, final, *refs):
    *blocks, xs, part, sums, load_hi, load_lo, held, flip_hi, flip_lo = refs
    if begun:
        *blocks, before, sums_before = blocks
    funds, width = part.shape
    total = load_hi.shape[0]
    at = 0
    extra = sums_before[...] if begun else jnp.zeros((8, funds), F32)
    for block in blocks:
        for b in range(block.shape[0]):
            load_hi[at : at + secs, :], load_lo[at : at + secs, :] = halves(block[b, 0:secs, :])
            held[at : at + secs, :] = block[b, secs : 2 * secs, :]
            extra = extra + block[b, 2 * secs : 2 * secs + 8, :]
            at += secs
    sums[...] = extra
    for g in range(0, total, 128):
        flip_hi[:, g : g + 128], flip_lo[:, g : g + 128] = halves(jnp.transpose(held[g : g + 128, :]))
    if final:
        row = lax.broadcasted_iota(jnp.int32, (128, funds), 0)
        fixed = jnp.transpose(jnp.where(row == 0, extra[6:7, :], 0.0))[:, 0:1]
    step = min(256, width)
    group = min(512, total)

    def exposed(c, g):
        cut = slice(first + c, first + c + step)
        x_hi, x_lo = (xs[i, :, cut] if year == 0 else xs[year - 1, i, :, cut] for i in range(2))
        lh, ll = load_hi[g : g + group, :], load_lo[g : g + group, :]
        return dot(jnp.concatenate([lh, lh], 1), jnp.concatenate([x_hi, x_lo], 0)) + dot(ll, x_hi)

    spots = [(c, g) for c in range(0, width, step) for g in range(0, total, group)]
    ahead = exposed(*spots[0])
    for i, (c, g) in enumerate(spots):
        now = ahead
        ahead = exposed(*spots[i + 1]) if i + 1 < len(spots) else None
        t_hi, t_lo = halves(jnp.tanh(now))
        fh, fl = flip_hi[:, g : g + group], flip_lo[:, g : g + group]
        new = 0.25 * dot(jnp.concatenate([fh, fh, fl], 1), jnp.concatenate([t_hi, t_lo, t_hi], 0))
        acc = new if g == 0 else acc + new
        if g + group == total:
            if begun:
                acc = acc + before[:, first + c : first + c + step]
            part[:, c : c + step] = acc + fixed if final else acc


def own_columns(me_ref, declared, first, out):
    paths, funds = out.shape
    width = declared.shape[1]
    spot = lax.broadcasted_iota(jnp.int32, (paths, width), 1) + first
    pick = spot == lax.broadcasted_iota(jnp.int32, (paths, width), 0) + me_ref[0] * paths
    pick = pick.astype(F32).astype(BF16)
    one, rest = declared.astype(BF16), declared - declared.astype(BF16).astype(F32)
    two, three = halves(rest)
    out[...] = dot(pick, one, ROW) + dot(pick, two, ROW) + dot(pick, three, ROW)


def rates_body(first, me, declared, out):
    own_columns(me, declared[...], first, out)


def slice_spot(me, order, slice_funds):
    core = (me & 1) ^ (order >> 1)
    side = ((me >> (1 + core)) & 1) ^ (order & 1)
    return pl.multiple_of((2 * core + side) * slice_funds, slice_funds)


def advance(step, got, base, guar, draw, asset, liab):
    wide = lambda v: jnp.concatenate([v] * (step // 128), 1)
    growth, credit = got[:, 0:step], jnp.maximum(got[:, step:], wide(guar))
    lapse = jnp.minimum(wide(base) * (0.5 + draw.astype(F32)) * jnp.exp(5.0 * (growth - credit)), 0.5)
    stay = 1.0 - lapse
    return asset * (1.0 + growth) * stay, liab * (1.0 + credit) * stay


def table_of(growth, declared):
    g_hi, g_lo = halves(growth)
    d_hi, d_lo = halves(declared)
    return jnp.concatenate([jnp.concatenate([g_hi, d_hi], 1), jnp.concatenate([g_lo, d_lo], 1)], 0)


def own_body(slice_funds, first, me, part, peer, *refs):
    totals, out = refs[:-1], refs[-1]
    rows = pl.ds(slice_spot(me[0], 0, slice_funds), slice_funds)
    cut = slice(first, first + out.shape[1])
    growth = part[rows, cut] + peer[rows, cut]
    asset, liab = totals[0][0], totals[0][1]
    for t in totals[1:]:
        asset, liab = asset + t[0], liab + t[1]
    out[...] = rate(asset * (1.0 + growth) / liab)


STEP, ROWS = 256, 512


def year_body(year, first, last, slice_funds, *refs):
    refs = list(refs)
    me = refs.pop(0)
    if year == 0:
        mine, other = refs.pop(0), refs.pop(0)
    else:
        slices = [refs.pop(0) for _ in range(4)]
    part, peer = refs.pop(0), refs.pop(0)
    draws, member, wides = refs.pop(0), refs.pop(0), refs.pop(0)
    held = [refs.pop(0) for _ in range(2 if year else 0)]
    lead = 0
    copies = []
    if last and first:
        half_a, half_l, *earlier, out_a, out_l, out_r, declared, buf_a, buf_l, rates, sem = refs
        for k, (half, out) in enumerate(((half_a, out_a), (half_l, out_l))):
            copies.append(pltpu.make_async_copy(half, out.at[:, 0:first], sem.at[k, 0]))
            copies[-1].start()
    elif last:
        out_a, out_l, own, declared = refs
    else:
        member_t = refs.pop(0)
        out_a, out_l, out_s, declared, acc = refs
    funds, width = declared.shape
    count = member.shape[1]
    if year == 0:
        sums = mine[...] + other[...]
        row = lax.broadcasted_iota(jnp.int32, (128, funds), 0)
        start_a = sums[0:1, :] + sums[1:2, :] + sums[2:3, :]
        start_l = sums[3:4, :] + sums[4:5, :] + sums[5:6, :]
        both = jnp.where(row == 0, start_a, jnp.where(row == 1, start_l, 0.0))
        both = jnp.transpose(both)
        ratio = both[:, 0:1] / both[:, 1:2]
        declared[...] = rate(ratio * (1.0 + (part[...] + peer[...])))
    else:
        lead = first
        for o in range(4):
            declared[pl.ds(slice_spot(me[0], o, slice_funds), slice_funds), :] = slices[o][...]
    if last and first:
        own_columns(me, declared[...], first, rates.at[year])
        rates[year] = rates[year] + earlier[2 * year][...]
        for y in range(year):
            rates[y] = earlier[2 * y][...] + earlier[2 * y + 1][...]
        copies.append(pltpu.make_async_copy(rates, out_r, sem.at[2, 0]))
        copies[-1].start()

    def gathered(c):
        there = slice(lead + c, lead + c + STEP)
        table = table_of(part[:, there] + peer[:, there], declared[:, c : c + STEP])
        return [dot(member[year, r : r + ROWS, :], table) for r in range(0, count, ROWS)]

    ahead = gathered(0)
    for c in range(0, width, STEP):
        cut = slice(c, c + STEP)
        now = ahead
        ahead = gathered(c + STEP) if c + STEP < width else None
        sum_a = sum_l = None
        for r in range(0, count, ROWS):
            rows = slice(r, r + ROWS)
            if year == 0:
                years = member.shape[0]
                asset = jnp.concatenate([wides[2 * years, rows, :]] * (STEP // 128), 1)
                liab = jnp.concatenate([wides[2 * years + 1, rows, :]] * (STEP // 128), 1)
            else:
                asset, liab = held[0][rows, cut], held[1][rows, cut]
            asset, liab = advance(
                STEP, now[r // ROWS], wides[2 * year, rows, :], wides[2 * year + 1, rows, :],
                draws[year, rows, first + c : first + c + STEP], asset, liab,
            )
            if last and first:
                buf_a[c // STEP, rows, :] = asset
                buf_l[c // STEP, rows, :] = liab
            else:
                out_a[rows, cut] = asset
                out_l[rows, cut] = liab
            if not last:
                a_hi, a_lo = halves(asset)
                l_hi, l_lo = halves(liab)
                ma, ml = member_t[year + 1, :, rows], member_t[0, :, rows]
                add_a = dot(jnp.concatenate([ma, ma], 1), jnp.concatenate([a_hi, a_lo], 0))
                add_l = dot(jnp.concatenate([ml, ml], 1), jnp.concatenate([l_hi, l_lo], 0))
                sum_a = add_a if sum_a is None else sum_a + add_a
                sum_l = add_l if sum_l is None else sum_l + add_l
        if last and first:
            for buf, out, k in ((buf_a, out_a, 0), (buf_l, out_l, 1)):
                copy = pltpu.make_async_copy(
                    buf.at[c // STEP], out.at[:, first + c : first + c + STEP], sem.at[k, 1 + c // STEP]
                )
                copy.start()
                copies.append(copy)
        elif not last:
            acc[0, :, cut] = sum_a
            acc[1, :, cut] = sum_l
    if last and not first:
        own_columns(me, declared[...], first, own)
    for copy in copies:
        copy.wait()
    if not last:
        for o in range(4):
            for v in range(2):
                spot = pl.ds(slice_spot(me[0], o, slice_funds), slice_funds)
                out_s[o // 2, o % 2, v] = acc[v, spot, :]


def local(
    shocks,
    loadings,
    sec_drift,
    holdings,
    fund_of,
    product_type,
    term_years,
    asset_start,
    liab_start,
    base_lapse,
    guarantee,
    lapse_draw,
):
    years, _, paths = shocks.shape
    secs, funds = holdings.shape
    count = asset_start.shape[0]
    n = lax.axis_size("pol")
    me = lax.axis_index("pol")
    me_ref = me.astype(jnp.int32).reshape(1)
    slice_funds = funds // 4
    owned = paths // n
    half = paths // 2
    draws = lapse_draw.transpose(1, 0, 2)
    line = lambda v: v.reshape(1, count)
    fund, kind, term = line(fund_of), line(product_type), line(term_years)
    asset, liab = line(asset_start), line(liab_start)

    sources = [loadings, holdings, sec_drift.reshape(1, secs), fund, term, asset, liab, kind]
    sources += [base_lapse.reshape(1, -1), guarantee.reshape(1, -1)]
    block, lines = call(
        pack_body,
        [shaped(2 * secs + 8, funds), shaped(8, count)],
        [SMEM] + [HBM] * 10,
        "pack",
        10**6,
        10**5,
        scratch=[pltpu.VMEM(v.shape, v.dtype) for v in sources] + [pltpu.SemaphoreType.DMA((10,))],
        limit=60,
    )(me_ref, *sources)
    far = far_offsets()
    came = swap(block[None], far[-1])
    member_t, member, wides, x_now, x_later, block = call(
        columns_body,
        [
            shaped(years, funds, count, dtype=BF16),
            shaped(years, count, 2 * funds, dtype=BF16),
            shaped(2 * years + 2, count, 128),
            shaped(2, *shocks.shape[1:], dtype=BF16),
            shaped(years - 1, 2, *shocks.shape[1:], dtype=BF16),
            shaped(1, *block.shape),
        ],
        [VMEM, VMEM, HBM],
        "columns",
        10**6,
        4 * 10**6,
        scratch=[pltpu.VMEM(shocks.shape, F32), pltpu.SemaphoreType.DMA],
        limit=8,
    )(lines, block, shocks)
    came, block = lax.optimization_barrier((came, block))
    block = jnp.concatenate([block, came])
    for o in reversed(far[:-1]):
        block = jnp.concatenate([block, swap(block, o)])
    blocks = [block] + [swap(block, o) for o in SQUARE]

    def returns(year, first, width, blocks, xs, before=(), final=True):
        total = secs * sum(b.shape[0] for b in blocks)
        return call(
            functools.partial(returns_body, year, first, secs, len(before) > 0, final),
            [shaped(funds, width), shaped(8, funds)],
            [VMEM] * (len(blocks) + len(before) + 1),
            "returns",
            scratch=[pltpu.VMEM((total, funds), BF16)] * 2
            + [pltpu.VMEM((total, funds), F32)]
            + [pltpu.VMEM((funds, total), BF16)] * 2,
            limit=8 * max(1, min(6, total // 512)),
        )(*blocks, *before, xs)

    before = ()
    for b in blocks[:-1]:
        before = returns(0, 0, paths, [b], x_now, before, False)
    firsts = [returns(0, h * half, half, blocks[-1:], x_now, before) for h in range(2)]
    sums = firsts[0][1]
    part = [p for p, _ in firsts]
    peer = [swap(p, 1) for p in part]
    other_sums = swap(sums, 1)

    later = {0: (part, peer)}
    others = []
    rates = [[None, None] for _ in range(years)]
    final = []

    def advance_half(h):
        first = h * half
        head, state = [sums, other_sums], []
        other = yield sums
        for year in range(years):
            last = year + 1 == years
            pair = [v[h] for v in later[0]] if year == 0 else list(later[year])
            ins = [me_ref] + tie(head, other) + pair + [draws, member, wides] + state
            specs = [SMEM] + [VMEM] * (len(ins) - 1)
            scratch = [pltpu.VMEM((funds, half), F32)]
            if last and h:
                tiles = half // STEP
                out = [shaped(count, paths), shaped(count, paths), shaped(years, owned, funds)]
                out_specs = [ANY] * 3
                scratch += [pltpu.VMEM((tiles, count, STEP), F32)] * 2
                scratch += [pltpu.VMEM((years, owned, funds), F32)]
                scratch += [pltpu.SemaphoreType.DMA((3, 1 + tiles))]
                before = final[:2] + [v for rs in rates for v in rs if v is not None]
                ins += before
                specs += [VMEM] * len(before)
            elif last:
                out = [shaped(count, half), shaped(count, half), shaped(owned, funds)]
                out_specs = [VMEM] * 3
            else:
                ins.append(member_t)
                specs.append(VMEM)
                out = [shaped(count, half)] * 2
                out += [shaped(2, 2, 2, slice_funds, half), shaped(funds, half)]
                out_specs = [VMEM] * 4
                scratch = [pltpu.VMEM((2, funds, half), F32)]
            result = call(
                functools.partial(year_body, year, first, last, slice_funds),
                out,
                specs,
                "year",
                flops=2 * 2 * count * 2 * funds * half,
                moved=20 * count * half,
                scratch=scratch,
                out_specs=out_specs,
                limit=10,
            )(*ins)
            if last:
                final[:] = result
                rates[year][h] = result[2]
                yield result[2]
                return
            state, share, declared = list(result[:2]), result[2], result[3]
            if year == 0 and h == 1:
                others.append(swap(jnp.concatenate(tie(blocks, share)), 1))
            other = yield share
            held = share[0] + tie(swap(share[1], 1), other)
            other = yield held
            came = tie(swap(held[1], *FIRST), other)
            if h == 0:
                made = returns(year + 1, 0, paths, blocks, tie(x_later, held))[0]
                came, made, ready = lax.optimization_barrier((came, made, list(others)))
                later[year + 1] = [made]
            held = held[0] + came
            rates[year][h] = call(
                functools.partial(rates_body, first),
                shaped(owned, funds),
                [SMEM, VMEM],
                "rates",
                limit=4,
            )(me_ref, tie(declared, held))
            other = yield held
            *steps, closing = list(FULL) + [(o,) for o in far[1:]]
            for i, step in enumerate(steps):
                came = tie(swap(held, *step), other)
                if i == 0:
                    came, rates[year][h] = lax.optimization_barrier((came, rates[year][h]))
                if i == 0 and h == 0:
                    made = returns(year + 1, 0, paths, ready, tie(x_later, held))[0]
                    came, made = lax.optimization_barrier((came, made))
                    later[year + 1].append(made)
                held = held + came
                other = yield held
            own = call(
                functools.partial(own_body, slice_funds, first),
                shaped(slice_funds, half),
                [SMEM] + [VMEM] * 4,
                "own",
                10**6,
                10**6,
                limit=2,
            )(me_ref, *later[year + 1], held, tie(swap(held, *closing), other))
            other = yield own
            near = tie(swap(own, *FIRST), other)
            other = yield near
            head = [own, near, swap(own, 1), swap(near, 1)]

    running = [advance_half(h) for h in range(2)]
    newest = [next(r) for r in running]
    while running:
        for h, r in enumerate(list(running)):
            try:
                newest[h] = r.send(newest[1 - h])
            except StopIteration:
                running.remove(r)
    assets, liability, credit = final
    return assets, liability, credit.transpose(0, 2, 1)


def solution(mesh):
    in_specs = (
        P("grp", None, None),
        P("pol", None),
        P("pol"),
        P("pol", None),
        P("pol", None),
        P("pol"),
        P("pol"),
        P("pol"),
        P("pol"),
        P(),
        P(),
        P("pol", "grp", None),
    )
    out_specs = (P("pol", "grp"), P("pol", "grp"), P("grp", None, "pol"))
    return jax.shard_map(local, mesh=mesh, in_specs=in_specs, out_specs=out_specs, check_vma=False)
```
